768 devices in a mesh: gx: 64 (over z_hi, y, core), gy: 12 (over z_lo, x).
Axes of the slice: x: 4, y: 8, z: 12 (z_hi: 4, z_lo: 3; z = z_hi * 3 + z_lo), core: 2. Of those that a mesh axis runs over, the one named last changes fastest.
Arguments:
- right_side: float32 [3, 128, 96, 384], P(None, 'gx', 'gy'), may hold values from -6 to 6
- face_mass: float32 [3, 128, 96, 384], P(None, 'gx', 'gy'), may hold values from 0.2 to 5
- edge_scale: float32 [3, 128, 96, 384], P(None, 'gx', None, 'gy'), may hold values from 0.1 to 0.5
- edge_mass: float32 [3, 128, 96, 384], P(None, 'gx', None, 'gy'), may hold values from 0.5 to 4
- node_scale: float32 [128, 96, 384], P('gx', None, 'gy'), may hold values from 0.1 to 0.4
Outputs:
- velocity: float32 [3, 128, 96, 384], P(None, 'gx', 'gy')
- edge_correction: float32 [3, 128, 96, 384], P(None, 'gx', None, 'gy')
The draws below stay inside these ranges and needn't reach their ends.
All inputs are finite; a program needn't handle non-finite values.
Results may differ from the reference program's by a relative error of at most 0.00002.
Values sent between devices are 32-bit elements; how exact they have to be, the bound alone decides.
A program may use at most 32 MiB of HBM per device.

```python
import math
import jax
import jax.numpy as jnp

NX = 128
NY = 96
NZ = 384


def block_levels(key, shape, shards, least, largest):
    gain = 1.0
    for position, blocks in shards:
        heights = jax.random.uniform(jax.random.fold_in(jax.random.fold_in(key, 6), position), (blocks,), jnp.float32, least / len(shards), largest / len(shards))
        gain = gain * jnp.repeat(jnp.exp(heights), shape[position] // blocks).reshape((-1,) + (1,) * (len(shape) - 1 - position))
    return gain


def scatter_about(stream_key, dims, scale, bound, cuts=(), held_as=jnp.bfloat16):
    level = block_levels(stream_key, dims, cuts, -0.22, 0.18) if cuts else 1.0
    result = jax.random.normal(stream_key, dims, jnp.float32) * scale * level
    return jnp.minimum(jnp.maximum(result, -bound), bound).astype(held_as)


def setup_inputs(seed: int = 0) -> dict:
    key_list = jax.random.split(jax.random.key(seed), 6)
    return {
        "right_side": scatter_about(key_list[0], (3, NX, NY, NZ), 1.0, 6.0, ((1, 64), (2, 12)), jnp.float32),
        "face_mass": jnp.clip(jnp.exp(math.log(5.0) - 3.218876 * jax.random.uniform(key_list[1], (3, NX, NY, NZ), jnp.float32) ** block_levels(key_list[1], (3, NX, NY, NZ), ((1, 64), (2, 12)), -0.2, 0.2)), 0.2, 5.0),
        "edge_scale": jnp.clip(jnp.exp(math.log(0.5) - 1.609438 * jax.random.uniform(key_list[2], (3, NX, NY, NZ), jnp.float32) ** block_levels(key_list[2], (3, NX, NY, NZ), ((1, 64), (3, 12)), -0.2, 0.2)), 0.1, 0.5),
        "edge_mass": jnp.clip(jnp.exp(math.log(4.0) - 2.0794415 * jax.random.uniform(key_list[3], (3, NX, NY, NZ), jnp.float32) ** block_levels(key_list[3], (3, NX, NY, NZ), ((1, 64), (3, 12)), -0.2, 0.2)), 0.5, 4.0),
        "node_scale": jnp.clip(jnp.exp(math.log(0.4) - 1.3862944 * jax.random.uniform(key_list[4], (NX, NY, NZ), jnp.float32) ** block_levels(key_list[4], (NX, NY, NZ), ((0, 64), (2, 12)), -0.2, 0.2)), 0.1, 0.4),
    }


grad_div_weight = 1.0
damping = 0.3


def forward(array_in, direction):
    return jnp.roll(array_in, -1, direction) - array_in


def backward(array_in, direction):
    return jnp.roll(array_in, 1, direction) - array_in


def apply_faces(flux, face_mass):
    divergence = forward(flux[0], 0) + forward(flux[1], 1) + forward(flux[2], 2)
    gradient = jnp.stack([backward(divergence, direction) for direction in range(3)])
    return face_mass * flux + grad_div_weight * gradient


def face_curl(edges):
    return jnp.stack([forward(edges[(component + 2) % 3], (component + 1) % 3) - forward(edges[(component + 1) % 3], (component + 2) % 3) for component in range(3)])


def curl_adjoint(faces):
    return jnp.stack([backward(faces[(component + 1) % 3], (component + 2) % 3) - backward(faces[(component + 2) % 3], (component + 1) % 3) for component in range(3)])


def gradient_adjoint(edges):
    return backward(edges[0], 0) + backward(edges[1], 1) + backward(edges[2], 2)


def node_gradient(nodal):
    return jnp.stack([forward(nodal, direction) for direction in range(3)])


def reference(right_side, face_mass, edge_scale, edge_mass, node_scale):
    diagonal = face_mass + 2.0 * grad_div_weight
    sweep_one = damping * right_side / diagonal
    sweep_two = sweep_one + damping * (right_side - apply_faces(sweep_one, face_mass)) / diagonal
    residual = right_side - apply_faces(sweep_two, face_mass)
    edge_residual = curl_adjoint(residual)
    smoothed = edge_scale * edge_residual
    potential = node_scale * (-gradient_adjoint(edge_mass * smoothed))
    edge_correction = smoothed + node_gradient(potential)
    corrected = sweep_two + face_curl(smoothed)
    velocity = corrected + damping * (right_side - apply_faces(corrected, face_mass)) / diagonal
    return velocity, edge_correction
```

```python
import functools

import jax
import jax.numpy as jnp
from jax import lax
from jax.experimental import pallas as pl
from jax.experimental.pallas import tpu as pltpu
from jax.sharding import PartitionSpec as P

MESH = pl.DeviceIdType.MESH
grad_div_weight = 1.0
damping = 0.3


def z_up(a):
    return pltpu.roll(a, a.shape[-1] - 1, axis=a.ndim - 1)


def z_down(a):
    return pltpu.roll(a, 1, axis=a.ndim - 1)


def y_up(a):
    return pltpu.roll(a, a.shape[-2] - 1, axis=a.ndim - 2)


def y_down(a):
    return pltpu.roll(a, 1, axis=a.ndim - 2)


def half_turn(a):
    return pltpu.roll(a, 4, axis=a.ndim - 2)


def sublane(shape):
    return lax.broadcasted_iota(jnp.int32, shape, len(shape) - 2)


def pack_halves(parts, upper):
    low = sublane(parts[0].shape) < 4
    packed = []
    for i in range(0, len(parts), 2):
        a = parts[i]
        b = half_turn(parts[i + 1] if i + 1 < len(parts) else a)
        packed.append(jnp.where(low, b, a) if upper else jnp.where(low, a, b))
    return packed


def halo_tiles(from_below, from_above, i):
    a, b = from_below[i // 2], from_above[i // 2]
    low = sublane(a.shape) < 4
    if i % 2 == 0:
        return jnp.where(low, b, a)
    return half_turn(jnp.where(low, a, b))


def kernel(n_gx, n_gy, r_ref, fm_ref, es_ref, em_ref, ns_ref, vel_ref, ec_ref,
           x_right, x_left, y_upper, y_lower, cr_upper, cr_lower, cl_upper, cl_lower, edge_out, back_out,
           in_left, in_right, in_below, in_above, in_cl_below, in_cl_above, in_cr_below, in_cr_above,
           edge_in, back_in, faced, ef_right, ef_left, in_ef_left, in_ef_right,
           res_right, res_left, in_res_left, in_res_right, s2_ref, div2_ref, res_ref, send_sem, recv_sem):
    gx, gy = lax.axis_index("gx"), lax.axis_index("gy")

    def at(dx, dy):
        return (lax.rem(gx + dx + n_gx, n_gx), lax.rem(gy + dy + n_gy, n_gy))

    barrier = pltpu.get_barrier_semaphore()
    greeted = [at(0, j) for j in range(1, n_gy)] + [at(a, b) for a in (1, -1) for b in (-1, 0, 1)]
    for peer in greeted:
        pl.semaphore_signal(barrier, inc=1, device_id=peer, device_id_type=MESH)

    def message(index, src, dst, peer):
        return pltpu.make_async_remote_copy(
            src_ref=src, dst_ref=dst, send_sem=send_sem.at[index], recv_sem=recv_sem.at[index],
            device_id=peer, device_id_type=MESH)

    r = [[r_ref[c, p] for p in range(2)] for c in range(3)]
    fm = [[fm_ref[c, p] for p in range(2)] for c in range(3)]
    s1 = [[damping * r[c][p] / (fm[c][p] + 2.0 * grad_div_weight) for p in range(2)] for c in range(3)]
    to_right = [r[0][1], r[1][1], r[2][1], fm[0][1], fm[1][1], fm[2][1], s1[0][0], s1[1][0], s1[2][0]]
    to_left = [r[0][0], fm[0][0], s1[1][0], s1[2][0], s1[0][1]]
    own = [f[c][p] for f in (r, fm) for c in range(3) for p in range(2)]
    for ref, parts in ((x_right, to_right), (x_left, to_left),
                       (y_upper, pack_halves(own, True)), (y_lower, pack_halves(own, False)),
                       (cr_upper, pack_halves(to_right, True)), (cr_lower, pack_halves(to_right, False)),
                       (cl_upper, pack_halves(to_left, True)), (cl_lower, pack_halves(to_left, False))):
        for i, part in enumerate(parts):
            ref[i] = part

    rows, width = es_ref.shape[2], es_ref.shape[3]
    low96 = sublane((rows, width)) % 8 < 4
    for a in range(7):
        windows = []
        for p in range(2):
            field = es_ref[a, p] if a < 3 else em_ref[a - 3, p] if a < 6 else ns_ref[p]
            after = jnp.concatenate([field[8:], field[:8]], axis=0)
            before = jnp.concatenate([field[rows - 8:], field[:rows - 8]], axis=0)
            windows += [field, jnp.where(low96, after, before)]
        edge_out[:, a] = jnp.concatenate(windows, axis=1).reshape(n_gy, 8, 4 * width)

    pl.semaphore_wait(barrier, len(greeted))

    first = [
        message(4, cr_upper, in_cl_below, at(1, 1)), message(5, cr_lower, in_cl_above, at(1, -1)),
        message(6, cl_upper, in_cr_below, at(-1, 1)), message(7, cl_lower, in_cr_above, at(-1, -1)),
        message(0, x_right, in_left, at(1, 0)), message(1, x_left, in_right, at(-1, 0)),
        message(2, y_upper, in_below, at(0, 1)), message(3, y_lower, in_above, at(0, -1)),
    ]
    for copy in first:
        copy.start()
    exchange = []
    for j in range(1, n_gy):
        peer = at(0, j)
        exchange.append(message(7 + j, edge_out.at[peer[1]], edge_in.at[gy], peer))
    for copy in exchange:
        copy.start()
    edge_in[gy] = edge_out[gy]

    for copy in exchange:
        copy.wait_recv()
    lane4 = lax.broadcasted_iota(jnp.int32, (8, 128), 1) // width
    for p in range(2):
        for a in range(7):
            for h in range(2):
                q = 2 * p + h
                for m in range(3):
                    tile = None
                    for jj in range(4):
                        piece = edge_in[4 * m + jj, a]
                        if jj != q:
                            piece = pltpu.roll(piece, (width * (jj - q)) % 128, axis=1)
                        tile = piece if tile is None else jnp.where(lane4 == jj, piece, tile)
                    faced[p, a, 8 * h:8 * h + 8, 128 * m:128 * m + 128] = tile
    sub = sublane((8, r_ref.shape[3]))
    for ref, p, count in ((ef_right, 1, 4), (ef_left, 0, 7)):
        for a in range(count):
            ref[a] = faced[p, a, 0:8]
        for base in range(0, count, 4):
            tile = None
            for i in range(min(4, count - base)):
                piece = faced[p, base + i, 8:16]
                piece = piece if i == 0 else pltpu.roll(piece, 2 * i, axis=0)
                tile = piece if i == 0 else jnp.where((sub == 2 * i) | (sub == 2 * i - 1), piece, tile)
            ref[count + base // 4] = tile
    edge_halo = [message(19, ef_right, in_ef_left, at(1, 0)), message(20, ef_left, in_ef_right, at(-1, 0))]
    for copy in edge_halo:
        copy.start()

    for copy in first:
        copy.wait_recv()

    def joined(own_part, halo):
        return jnp.concatenate([own_part, halo], axis=0)

    def left(i):
        return joined(in_left[i], halo_tiles(in_cl_below, in_cl_above, i))

    def right(i):
        return joined(in_right[i], halo_tiles(in_cr_below, in_cr_above, i))

    def mine(i, part):
        return joined(part, halo_tiles(in_below, in_above, i))

    rr = {(c, p): mine(2 * c + p, r_ref[c, p]) for c in range(3) for p in range(2)}
    ff = {(c, p): mine(6 + 2 * c + p, fm_ref[c, p]) for c in range(3) for p in range(2)}
    for c in range(3):
        rr[c, -1], ff[c, -1] = left(c), left(3 + c)
    rr[0, 2], ff[0, 2] = right(0), right(1)
    dd = {key: ff[key] + 2.0 * grad_div_weight for key in ff}
    ss = {key: damping * rr[key] / dd[key] for key in rr}
    for c in range(3):
        ss[c, -2] = left(6 + c)
    ss[1, 2], ss[2, 2], ss[0, 3] = right(2), right(3), right(4)

    def divergence(u, p):
        return (u[0, p + 1] - u[0, p]) + (y_up(u[1, p]) - u[1, p]) + (z_up(u[2, p]) - u[2, p])

    def back_of(div, c, p):
        shifted = div[p - 1] if c == 0 else y_down(div[p]) if c == 1 else z_down(div[p])
        return shifted - div[p]

    def apply_faces(u, div, c, p):
        return ff[c, p] * u[c, p] + grad_div_weight * back_of(div, c, p)

    div1 = {p: divergence(ss, p) for p in range(-2, 3)}
    tt = {key: ss[key] + damping * (rr[key] - apply_faces(ss, div1, *key)) / dd[key] for key in rr}
    div2 = {p: divergence(tt, p) for p in range(-1, 2)}
    res = {(c, p): rr[c, p] - apply_faces(tt, div2, c, p) for c in range(3) for p in range(2)}

    def pack_three_rows(parts):
        packed = []
        middle = (sub >= 2) & (sub <= 4)
        for i in range(0, len(parts), 2):
            a = parts[i][8:16]
            packed.append(jnp.where(middle, half_turn(parts[i + 1][8:16]), a) if i + 1 < len(parts) else a)
        return packed

    right_going = [res[1, 0], res[2, 0], res[0, 1], res[1, 1], res[2, 1]]
    left_going = [res[0, 0], res[1, 0], res[2, 0]]
    for ref, parts in ((res_right, right_going), (res_left, left_going)):
        for i, part in enumerate([a[0:8] for a in parts] + pack_three_rows(parts)):
            ref[i] = part
    second = [message(21, res_right, in_res_left, at(1, 0)), message(22, res_left, in_res_right, at(-1, 0))]
    for copy in second:
        copy.start()
    for copy in edge_halo:
        copy.wait_recv()
    for copy in second:
        copy.wait_recv()

    def res_halo(ref, count, i):
        tile = ref[count + i // 2]
        return joined(ref[i], half_turn(tile) if i % 2 else tile)

    for i, key in enumerate(((1, -2), (2, -2), (0, -1), (1, -1), (2, -1))):
        res[key] = res_halo(in_res_left, 5, i)
    for c in range(3):
        res[c, 2] = res_halo(in_res_right, 3, c)

    def ef_halo(ref, count, i):
        tile = ref[count + i // 4]
        return joined(ref[i], pltpu.roll(tile, 8 - 2 * (i % 4), axis=0) if i % 4 else tile)

    edge = {(a, p): faced[p, a] for a in range(7) for p in range(2)}
    for a in range(4):
        edge[a, -1] = ef_halo(in_ef_left, 4, a)
    for a in range(7):
        edge[a, 2] = ef_halo(in_ef_right, 7, a)

    def shift_down(u, c, p, direction):
        return u[c, p - 1] if direction == 0 else y_down(u[c, p]) if direction == 1 else z_down(u[c, p])

    def edge_residual(a, p):
        b, c = (a + 1) % 3, (a + 2) % 3
        return (shift_down(res, b, p, c) - res[b, p]) - (shift_down(res, c, p, b) - res[c, p])

    sm = {(a, p): edge[a, p] * edge_residual(a, p) for p in range(-1, 3) for a in range(3)}
    ww = {(a, p): edge[3 + a, p] * sm[a, p] for p in range(-1, 3) for a in range(3) if p >= 0 or a == 0}
    pot = {}
    for p in range(3):
        adjoint = ((ww[0, p - 1] - ww[0, p]) + (y_down(ww[1, p]) - ww[1, p])) + (z_down(ww[2, p]) - ww[2, p])
        pot[p] = edge[6, p] * -adjoint
    lane = lax.broadcasted_iota(jnp.int32, (8, 128), 1) // width
    corr = []
    for c in range(3):
        for p in range(2):
            ahead = pot[p + 1] if c == 0 else y_up(pot[p]) if c == 1 else z_up(pot[p])
            corr.append((sm[c, p] + (ahead - pot[p]))[0:8])
    for k in range(n_gy):
        for t in range(2):
            tile = None
            for i, field in enumerate(corr[4 * t:4 * t + 4]):
                piece = field[:, 128 * (k // 4):128 * (k // 4) + 128]
                turn = (i - k) % 4
                piece = pltpu.roll(piece, width * turn, axis=1) if turn else piece
                tile = piece if tile is None else jnp.where(lane == i, piece, tile)
            back_out[k, t] = tile
    returned = []
    for j in range(1, n_gy):
        peer = at(0, j)
        returned.append(message(22 + j, back_out.at[peer[1]], back_in.at[gy], peer))
    for copy in returned:
        copy.start()
    back_in[gy] = back_out[gy]

    def shift_up(u, c, p, direction):
        return u[c, p + 1] if direction == 0 else y_up(u[c, p]) if direction == 1 else z_up(u[c, p])

    def curl(c, p):
        a, b = (c + 1) % 3, (c + 2) % 3
        return (shift_up(sm, b, p, a) - sm[b, p]) - (shift_up(sm, a, p, b) - sm[a, p])

    new = {key: tt[key] + curl(*key) for key in tt}
    div3 = {p: divergence(new, p) for p in range(-1, 2)}
    for c in range(3):
        for p in range(2):
            key = (c, p)
            out = new[key] + damping * (rr[key] - apply_faces(new, div3, c, p)) / dd[key]
            vel_ref[c, p] = out[0:8]

    for copy in returned:
        copy.wait_recv()
    for t in range(2):
        whole = back_in[:, t].reshape(rows, 128)
        for i in range(4 if t == 0 else 2):
            c, p = divmod(4 * t + i, 2)
            piece = whole if i == 0 else pltpu.roll(whole, 128 - width * i, axis=1)
            ec_ref[c, p] = piece[:, :width]
    for copy in first + exchange + edge_halo + second + returned:
        copy.wait_send()


def on_device(right_side, face_mass, edge_scale, edge_mass, node_scale):
    n_gx, n_gy = lax.axis_size("gx"), lax.axis_size("gy")
    nz = right_side.shape[3]

    def tiles(*lead):
        return pltpu.VMEM((*lead, 8, nz), jnp.float32)

    def packed(*lead):
        return pltpu.VMEM((*lead, 8, 128), jnp.float32)

    vmem = pl.BlockSpec(memory_space=pltpu.VMEM)
    count = 23 + n_gy - 1
    return pl.pallas_call(
        functools.partial(kernel, n_gx, n_gy),
        out_shape=(jax.ShapeDtypeStruct(right_side.shape, jnp.float32),
                   jax.ShapeDtypeStruct(edge_scale.shape, jnp.float32)),
        in_specs=[vmem] * 5,
        out_specs=(vmem, vmem),
        scratch_shapes=[
            tiles(9), tiles(5), tiles(6), tiles(6), tiles(5), tiles(5), tiles(3), tiles(3),
            packed(n_gy, 7), packed(n_gy, 2),
            tiles(9), tiles(5), tiles(6), tiles(6), tiles(5), tiles(5), tiles(3), tiles(3),
            packed(n_gy, 7), packed(n_gy, 2),
            pltpu.VMEM((2, 7, 16, nz), jnp.float32),
            tiles(5), tiles(9), tiles(5), tiles(9),
            tiles(8), tiles(5), tiles(8), tiles(5),
            tiles(1), tiles(1), tiles(1),
            pltpu.SemaphoreType.DMA((count,)), pltpu.SemaphoreType.DMA((count,)),
        ],
        compiler_params=pltpu.CompilerParams(
            collective_id=0, has_side_effects=True, vmem_limit_bytes=32 * 1024 * 1024),
    )(right_side, face_mass, edge_scale, edge_mass, node_scale)


def solution(mesh):
    placed = (
        P(None, "gx", "gy", None),
        P(None, "gx", "gy", None),
        P(None, "gx", None, "gy"),
        P(None, "gx", None, "gy"),
        P("gx", None, "gy"),
    )
    return jax.shard_map(
        on_device,
        mesh=mesh,
        in_specs=placed,
        out_specs=(P(None, "gx", "gy", None), P(None, "gx", None, "gy")),
        check_vma=False,
    )
```

```python
import functools

import jax
import jax.numpy as jnp
from jax import lax
from jax.experimental import pallas as pl
from jax.experimental.pallas import tpu as pltpu
from jax.sharding import PartitionSpec as P

MESH = pl.DeviceIdType.MESH
grad_div_weight = 1.0
damping = 0.3


def up(a, axis):
    return pltpu.roll(a, a.shape[axis] - 1, axis=axis)


def down(a, axis):
    return pltpu.roll(a, 1, axis=axis)


def half_turn(a):
    return pltpu.roll(a, 4, axis=0)


def sublane(shape):
    return lax.broadcasted_iota(jnp.int32, shape, len(shape) - 2)


def shift_up(u, c, p, direction, axes):
    return u[c, p + 1] if direction == 0 else up(u[c, p], axes[direction - 1])


def shift_down(u, c, p, direction, axes):
    return u[c, p - 1] if direction == 0 else down(u[c, p], axes[direction - 1])


FACE = (0, 1)
EDGE = (1, 0)


def curl(u, c, p, axes):
    a, b = (c + 1) % 3, (c + 2) % 3
    return (shift_up(u, b, p, a, axes) - u[b, p]) - (shift_up(u, a, p, b, axes) - u[a, p])


def curl_adjoint(g, a, p, axes):
    b, c = (a + 1) % 3, (a + 2) % 3
    return (shift_down(g, b, p, c, axes) - g[b, p]) - (shift_down(g, c, p, b, axes) - g[c, p])


def turn(a, by):
    return pltpu.roll(a, by % 8, axis=0) if by % 8 else a


def pack_rows(items):
    packed = []
    for base in range(0, len(items), 8):
        tile = None
        for slot, (a, row) in enumerate(items[base:base + 8]):
            piece = turn(a, slot - row)
            tile = piece if tile is None else jnp.where(sublane(a.shape) == slot, piece, tile)
        packed.append(tile)
    return packed


def with_rows(tile, *items):
    for ref, slot, row in items:
        piece = turn(ref[slot // 8], row - slot % 8)
        tile = piece if tile is None else jnp.where(sublane(piece.shape) == row, piece, tile)
    return tile


def joined(own_part, halo):
    return jnp.concatenate([own_part, halo], axis=0)


def kernel(n_gx, n_gy, r_hbm, fm_hbm, es_hbm, em_hbm, ns_hbm, vel_ref, ec_ref,
           r_ref, fm_ref, es_ref, em_ref, ns_ref,
           x_right, x_left, y_upper, y_lower, cr_upper, cr_lower, cl_upper, cl_lower,
           in_left, in_right, in_below, in_above, in_cl_below, in_cl_above, in_cr_below, in_cr_above,
           es_out, es_in, faced, ef_right, ef_left, in_ef_left, in_ef_right,
           e_left, e_right, e_next, e_prev, e_ca, e_cb, in_e_right, in_e_left, in_e_next, in_e_prev, in_e_ca, in_e_cb,
           res_right, res_left, res_upper, res_lower, rr_upper, rr_lower, rl_upper, rl_lower,
           in_res_left, in_res_right, in_res_below, in_res_above, in_rl_below, in_rl_above, in_rr_below, in_rr_above, win, in_win, in_win_right, in_win_left,
           load_sem, send_sem, recv_sem):
    gx, gy = lax.axis_index("gx"), lax.axis_index("gy")

    def at(dx, dy):
        return (lax.rem(gx + dx + n_gx, n_gx), lax.rem(gy + dy + n_gy, n_gy))

    barrier = pltpu.get_barrier_semaphore()
    greeted = [at(a, b) for a in (1, -1) for b in (-1, 0, 1)] + [at(0, j) for j in range(1, n_gy)]
    for peer in greeted:
        pl.semaphore_signal(barrier, inc=1, device_id=peer, device_id_type=MESH)
    loads = [pltpu.make_async_copy(src, dst, load_sem.at[i]) for i, (src, dst) in enumerate(
        ((r_hbm, r_ref), (fm_hbm, fm_ref), (es_hbm, es_ref), (em_hbm, em_ref), (ns_hbm, ns_ref)))]
    for load in loads:
        load.start()
    sent = []

    def message(src, dst, peer):
        index = len(sent)
        copy = pltpu.make_async_remote_copy(
            src_ref=src, dst_ref=dst, send_sem=send_sem.at[index], recv_sem=recv_sem.at[index],
            device_id=peer, device_id_type=MESH)
        sent.append(copy)
        copy.start()
        return copy

    for load in loads[:2]:
        load.wait()
    r = [[r_ref[c, p] for p in range(2)] for c in range(3)]
    fm = [[fm_ref[c, p] for p in range(2)] for c in range(3)]
    s1 = [[damping * r[c][p] / (fm[c][p] + 2.0 * grad_div_weight) for p in range(2)] for c in range(3)]
    known = [s1[0][1] - s1[0][0], up(s1[2][0], 1) - s1[2][0]]
    wide = sublane(known[0].shape)
    partial = known[0] + (jnp.where(wide == 7, 0.0, up(s1[1][0], 0)) - s1[1][0]) + known[1]
    to_right = [r[c][1] for c in range(3)] + [fm[c][1] for c in range(3)] + [partial]
    to_left = [r[0][0], fm[0][0], known[0] + known[1], s1[1][0]]
    cells = [(c, p) for c in range(3) for p in range(2)]
    for ref, parts in (
            (x_right, to_right), (x_left, to_left),
            (y_upper, pack_rows([(f[c][p], 7) for f in (r, fm) for c, p in cells] + [(s1[c][p], 6) for c, p in cells])),
            (y_lower, pack_rows([(f[p], 0) for f in (r[1], fm[1], s1[0], s1[2]) for p in range(2)]
                                + [(s1[1][p], 1) for p in range(2)])),
            (cr_upper, pack_rows([(s1[c][1], 7) for c in range(3)])),
            (cr_lower, pack_rows([(r[1][1], 0), (fm[1][1], 0), (s1[0][1], 0), (s1[2][1], 0), (s1[1][1], 1), (s1[1][0], 0)])),
            (cl_upper, pack_rows([(to_left[i], 7) for i in range(4)] + [(s1[0][0], 6)])),
            (cl_lower, pack_rows([(s1[1][0], 0), (s1[0][0], 0)]))):
        for i, part in enumerate(parts):
            ref[i] = part

    for load in loads[2:]:
        load.wait()
    nz, ny = es_ref.shape[2], es_ref.shape[3]

    def wrapped(field):
        return jnp.concatenate([field, field[:, :16], field[:, ny - 16:]], axis=1)

    es = {(c, p): wrapped(es_ref[c, p]) for c in range(3) for p in range(2)}
    em = {(c, p): wrapped(em_ref[c, p]) for c in range(3) for p in range(2)}
    ns = {p: wrapped(ns_ref[p]) for p in range(2)}
    both = {key: em[key] * es[key] for key in es}
    for i, field in enumerate([both[c, 0] for c in range(3)] + [ns[0]]):
        e_left[i] = field
    e_right[0] = both[0, 1]
    for i, field in enumerate([both[key] for key in cells] + [ns[0], ns[1]]):
        e_next[i] = field[0:8]
    for p in range(2):
        e_prev[p] = both[2, p][nz - 8:]
    e_ca[0] = both[2, 0][nz - 8:]
    e_cb[0] = both[0, 1][0:8]

    order = [(c, p) for p in range(2) for c in range(3)]
    sub = sublane((8, 128))
    halos = []
    for t in range(2):
        group = [es[key] for key in order[4 * t:4 * t + 4]]
        group += [group[0]] * (4 - len(group))
        turned = jnp.concatenate(group, axis=0).T
        es_out[:, t] = turned[:ny].reshape(n_gy, 8, 128)
        after = turned[8:ny + 8].reshape(n_gy, 8, 128)
        before = jnp.concatenate([turned[ny - 8:ny], turned[:ny - 8]], axis=0).reshape(n_gy, 8, 128)
        halos.append((after, before))
    for k in range(n_gy):
        first_halo = jnp.where(sub < 4, halos[0][0][k], halos[0][1][k])
        second_halo = half_turn(jnp.where(sub < 4, halos[1][0][k], halos[1][1][k]))
        es_out[k, 2] = jnp.where((sub == 3) | (sub == 4), second_halo, first_halo)

    pl.semaphore_wait(barrier, len(greeted))

    first = [
        message(cr_upper, in_cl_below, at(1, 1)), message(cr_lower, in_cl_above, at(1, -1)),
        message(cl_upper, in_cr_below, at(-1, 1)), message(cl_lower, in_cr_above, at(-1, -1)),
        message(x_left, in_right, at(-1, 0)), message(x_right, in_left, at(1, 0)),
        message(y_upper, in_below, at(0, 1)), message(y_lower, in_above, at(0, -1)),
    ]
    exchange = []
    for j in range(1, n_gy):
        peer = at(0, j)
        exchange.append(message(es_out.at[peer[1]], es_in.at[gy], peer))
    es_in[gy] = es_out[gy]
    edge_halo = [
        message(e_left, in_e_right, at(-1, 0)), message(e_right, in_e_left, at(1, 0)),
        message(e_next, in_e_next, at(0, -1)), message(e_prev, in_e_prev, at(0, 1)),
        message(e_ca, in_e_ca, at(-1, 1)), message(e_cb, in_e_cb, at(1, -1)),
    ]

    for copy in first:
        copy.wait_recv()

    rr, ff, dd, ss = {}, {}, {}, {}
    for i, (c, p) in enumerate(cells):
        above = c == 1
        rr[c, p] = joined(r_ref[c, p], with_rows(None, (in_below, i, 7), *[(in_above, p, 0)] * above))
        ff[c, p] = joined(fm_ref[c, p], with_rows(None, (in_below, 6 + i, 7), *[(in_above, 2 + p, 0)] * above))
    for c in range(3):
        rr[c, -1] = joined(in_left[c], with_rows(None, (in_cl_above, 0, 0)) if c == 1 else in_left[c])
        ff[c, -1] = joined(in_left[3 + c], with_rows(None, (in_cl_above, 1, 0)) if c == 1 else in_left[3 + c])
    rr[0, 2] = joined(in_right[0], with_rows(None, (in_cr_below, 0, 7)))
    ff[0, 2] = joined(in_right[1], with_rows(None, (in_cr_below, 1, 7)))
    for key in rr:
        dd[key] = ff[key] + 2.0 * grad_div_weight
        ss[key] = damping * rr[key] / dd[key]

    def more_rows(key, *items):
        ss[key] = joined(ss[key][0:8], with_rows(ss[key][8:16], *items))

    for i, (c, p) in enumerate(cells):
        more_rows((c, p), (in_below, 12 + i, 6), (in_above, (4, 8, 6)[c] + p, 1 if c == 1 else 0))
    for c in range(3):
        more_rows((c, -1), (in_cl_below, c, 7), (in_cl_above, (2, 4, 3)[c], 1 if c == 1 else 0))
    more_rows((0, 2), (in_cr_below, 4, 6), (in_cr_above, 1, 0))
    known = joined(in_right[2], with_rows(None, (in_cr_below, 2, 7)))
    second_flux = joined(in_right[3], with_rows(None, (in_cr_below, 3, 7), (in_cr_above, 0, 0)))

    def divergence(u, p):
        return (u[0, p + 1] - u[0, p]) + (up(u[1, p], 0) - u[1, p]) + (up(u[2, p], 1) - u[2, p])

    def apply_faces(u, div, c, p):
        shifted = div[p - 1] if c == 0 else down(div[p], c - 1)
        return ff[c, p] * u[c, p] + grad_div_weight * (shifted - div[p])

    div1 = {p: divergence(ss, p) for p in range(-1, 2)}
    div1[2] = known + (up(second_flux, 0) - second_flux)
    far = in_left[6]
    far = jnp.where(wide == 7, far + turn(in_cl_above[0], 2), far)
    div1[-2] = joined(far, far)
    tt = {key: ss[key] + damping * (rr[key] - apply_faces(ss, div1, *key)) / dd[key] for key in rr}
    div2 = {p: divergence(tt, p) for p in range(-1, 2)}
    res = {(c, p): rr[c, p] - apply_faces(tt, div2, c, p) for c in range(3) for p in range(2)}

    mine = {key: res[key][0:8] for key in res}
    for ref, parts in (
            (res_right, [mine[1, 0], mine[2, 0], mine[0, 1], mine[1, 1], mine[2, 1]]),
            (res_left, [mine[0, 0], mine[1, 0], mine[2, 0]]),
            (res_upper, pack_rows([(mine[key], 7) for key in cells] + [(mine[c, p], 6) for c in (0, 2) for p in range(2)])),
            (res_lower, pack_rows([(mine[key], 0) for key in cells])),
            (rr_upper, pack_rows([(mine[c, 1], 7) for c in range(3)])),
            (rr_lower, pack_rows([(mine[c, 1], 0) for c in range(3)] + [(mine[1, 0], 0)])),
            (rl_upper, pack_rows([(mine[c, 0], 7) for c in range(3)] + [(mine[0, 0], 6)])),
            (rl_lower, pack_rows([(mine[c, 0], 0) for c in range(2)]))):
        for i, part in enumerate(parts):
            ref[i] = part
    second = [
        message(rr_upper, in_rl_below, at(1, 1)), message(rr_lower, in_rl_above, at(1, -1)),
        message(rl_upper, in_rr_below, at(-1, 1)), message(rl_lower, in_rr_above, at(-1, -1)),
        message(res_right, in_res_left, at(1, 0)), message(res_left, in_res_right, at(-1, 0)),
        message(res_upper, in_res_below, at(0, 1)), message(res_lower, in_res_above, at(0, -1)),
    ]

    span = nz + 8
    lane = lax.broadcasted_iota(jnp.int32, (8, 128), 1)
    total = r_ref.shape[3]
    for k in range(n_gy):
        for p in range(2):
            tile = None
            for c in range(3):
                shift = (span * c - (nz * k - 4)) % total
                piece = (pltpu.roll(mine[c, p], shift, axis=1) if shift else mine[c, p])[:, :128]
                tile = piece if tile is None else jnp.where(lane >= span * c, piece, tile)
            win[k, p] = tile
    windows = []
    for j in range(n_gy):
        for side, p, dst in ((1, 1, in_win_left), (-1, 0, in_win_right)):
            peer = at(side, j)
            windows.append(message(win.at[peer[1], p], dst.at[gy], peer))
    for j in range(1, n_gy):
        peer = at(0, j)
        windows.append(message(win.at[peer[1]], in_win.at[gy], peer))
    in_win[gy] = win[gy]

    for copy in exchange:
        copy.wait_recv()
    lane4 = lane // nz
    for i, (c, p) in enumerate(order):
        t, q = divmod(i, 4)
        for m in range(total // 128):
            for h in range(2):
                tile = None
                for jj in range(4):
                    piece = es_in[4 * m + jj, 2 if h else t]
                    if jj != q:
                        piece = pltpu.roll(piece, (nz * (jj - q)) % 128, axis=1)
                    tile = piece if tile is None else jnp.where(lane4 == jj, piece, tile)
                faced[p, c, 8 * h:8 * h + 8, 128 * m:128 * m + 128] = half_turn(tile) if h and t else tile
    for ref, p, comps in ((ef_right, 1, (0, 1, 2)), (ef_left, 0, (1, 2))):
        tile = None
        for i, c in enumerate(comps):
            ref[i] = faced[p, c, 0:8]
            piece = faced[p, c, 8:16]
            piece = pltpu.roll(piece, 2 * i, axis=0) if i else piece
            tile = piece if tile is None else jnp.where((wide == 2 * i) | (wide == 2 * i - 1), piece, tile)
        ref[len(comps)] = tile
    scale_halo = [message(ef_right, in_ef_left, at(1, 0)), message(ef_left, in_ef_right, at(-1, 0))]

    for copy in second + scale_halo:
        copy.wait_recv()

    def ef_halo(ref, count, i):
        tile = ref[count]
        return joined(ref[i], pltpu.roll(tile, 8 - 2 * i, axis=0) if i else tile)

    for i, (c, p) in enumerate(cells):
        rows = [(in_res_below, i, 7), (in_res_above, i, 0)] + [(in_res_below, 6 + c + p, 6)] * (c != 1)
        res[c, p] = joined(mine[c, p], with_rows(None, *rows))
    res[1, -2] = joined(in_res_left[0], with_rows(None, (in_rl_above, 3, 0)))
    res[2, -2] = joined(in_res_left[1], in_res_left[1])
    for c in range(3):
        res[c, -1] = joined(in_res_left[2 + c], with_rows(None, (in_rl_below, c, 7), (in_rl_above, c, 0)))
        rows = [(in_rr_below, c, 7)] + [(in_rr_below, 3, 6)] * (c == 0) + [(in_rr_above, c, 0)] * (c < 2)
        res[c, 2] = joined(in_res_right[c], with_rows(None, *rows))
    scale = {(c, p): faced[p, c] for c in range(3) for p in range(2)}
    for c in range(3):
        scale[c, -1] = ef_halo(in_ef_left, 3, c)
    for c in range(1, 3):
        scale[c, 2] = ef_halo(in_ef_right, 2, c - 1)
    sm = {key: scale[key] * curl_adjoint(res, *key, FACE) for key in scale}
    new = {key: tt[key] + curl(sm, *key, FACE) for key in tt}
    div3 = {p: divergence(new, p) for p in range(-1, 2)}
    for c in range(3):
        for p in range(2):
            key = (c, p)
            out = new[key] + damping * (rr[key] - apply_faces(new, div3, c, p)) / dd[key]
            vel_ref[c, p] = out[0:8]

    for copy in edge_halo + windows:
        copy.wait_recv()
    g = {}
    for p, ref in ((-1, in_win_left), (0, None), (1, None), (2, in_win_right)):
        rows = (in_win[:, p] if ref is None else ref[...]).reshape(ny, 128)
        turned = jnp.concatenate([rows, rows[:16], rows[ny - 16:]], axis=0).T
        for c in range(3):
            g[c, p] = pltpu.roll(turned[span * c:span * c + span], span - 4, axis=0)
    low = sub < 4
    both = {}
    for i, (c, p) in enumerate(cells):
        halo = in_e_next[i]
        if c == 2:
            halo = jnp.where(low, halo, in_e_prev[p])
        both[c, p] = joined(wrapped(em_ref[c, p]) * wrapped(es_ref[c, p]), halo)
    node = {p: joined(wrapped(ns_ref[p]), in_e_next[6 + p]) for p in range(2)}
    both[0, -1] = joined(in_e_left[0], in_e_cb[0])
    for c in range(3):
        both[c, 2] = joined(in_e_right[c], in_e_ca[0])
    node[2] = joined(in_e_right[3], in_e_ca[0])
    edge_residual = {key: curl_adjoint(g, *key, EDGE) for key in both}
    ww = {key: both[key] * edge_residual[key] for key in both}
    pot = {}
    for p in range(3):
        adjoint = ((ww[0, p - 1] - ww[0, p]) + (down(ww[1, p], 1) - ww[1, p])) + (down(ww[2, p], 0) - ww[2, p])
        pot[0, p] = node[p] * -adjoint
    for c in range(3):
        for p in range(2):
            ahead = pot[0, p + 1] if c == 0 else up(pot[0, p], EDGE[c - 1])
            smoothed = wrapped(es_ref[c, p]) * edge_residual[c, p][:nz]
            ec_ref[c, p] = (smoothed + (ahead - pot[0, p])[:nz])[:, :ny]
    for copy in sent:
        copy.wait_send()


def on_device(right_side, face_mass, edge_scale, edge_mass, node_scale):
    n_gx, n_gy = lax.axis_size("gx"), lax.axis_size("gy")
    edge_scale, edge_mass, node_scale = (jnp.swapaxes(a, -1, -2) for a in (edge_scale, edge_mass, node_scale))
    total, nz = right_side.shape[3], edge_scale.shape[2]

    def own(a):
        return pltpu.VMEM(a.shape, jnp.float32)

    def rows(*lead):
        return pltpu.VMEM((*lead, 8, total), jnp.float32)

    def tile(*lead):
        return pltpu.VMEM((*lead, 8, 128), jnp.float32)

    def field(*lead):
        return pltpu.VMEM((*lead, nz, 128), jnp.float32)

    vmem = pl.BlockSpec(memory_space=pltpu.VMEM)
    arguments = (right_side, face_mass, edge_scale, edge_mass, node_scale)
    first = [rows(7), rows(4), rows(3), rows(2), rows(1), rows(1), rows(1), rows(1)]
    second = [rows(5), rows(3), rows(2), rows(1), rows(1), rows(1), rows(1), rows(1)]
    halo = [field(4), field(1), tile(8), tile(2), tile(1), tile(1)]
    count = 24 + 5 * n_gy - 2
    velocity, correction = pl.pallas_call(
        functools.partial(kernel, n_gx, n_gy),
        out_shape=(jax.ShapeDtypeStruct(right_side.shape, jnp.float32),
                   jax.ShapeDtypeStruct(edge_scale.shape, jnp.float32)),
        in_specs=[pl.BlockSpec(memory_space=pltpu.HBM)] * 5,
        out_specs=(vmem, vmem),
        scratch_shapes=[own(a) for a in arguments] + first + first + [
            tile(n_gy, 3), tile(n_gy, 3), pltpu.VMEM((2, 3, 16, total), jnp.float32),
            rows(4), rows(3), rows(4), rows(3)] + halo + halo + [
            *second, *second, tile(n_gy, 2), tile(n_gy, 2), tile(n_gy), tile(n_gy),
            pltpu.SemaphoreType.DMA((5,)),
            pltpu.SemaphoreType.DMA((count,)), pltpu.SemaphoreType.DMA((count,)),
        ],
        compiler_params=pltpu.CompilerParams(
            collective_id=0, has_side_effects=True, vmem_limit_bytes=60 * 1024 * 1024),
    )(*arguments)
    return velocity, jnp.swapaxes(correction, 2, 3)


def solution(mesh):
    placed = (
        P(None, "gx", "gy", None),
        P(None, "gx", "gy", None),
        P(None, "gx", None, "gy"),
        P(None, "gx", None, "gy"),
        P("gx", None, "gy"),
    )
    return jax.shard_map(
        on_device,
        mesh=mesh,
        in_specs=placed,
        out_specs=(P(None, "gx", "gy", None), P(None, "gx", None, "gy")),
        check_vma=False,
    )
```

```python
import functools

import jax
import jax.numpy as jnp
from jax import lax
from jax.experimental import pallas as pl
from jax.experimental.pallas import tpu as pltpu
from jax.sharding import PartitionSpec as P

MESH = pl.DeviceIdType.MESH
grad_div_weight = 1.0
damping = 0.3


def up(a, axis):
    return pltpu.roll(a, a.shape[axis] - 1, axis=axis)


def down(a, axis):
    return pltpu.roll(a, 1, axis=axis)


def half_turn(a):
    return pltpu.roll(a, 4, axis=0)


def sublane(shape):
    return lax.broadcasted_iota(jnp.int32, shape, len(shape) - 2)


def shift_up(u, c, p, direction, axes):
    return u[c, p + 1] if direction == 0 else up(u[c, p], axes[direction - 1])


def shift_down(u, c, p, direction, axes):
    return u[c, p - 1] if direction == 0 else down(u[c, p], axes[direction - 1])


FACE = (0, 1)
EDGE = (1, 0)


def curl(u, c, p, axes):
    a, b = (c + 1) % 3, (c + 2) % 3
    return (shift_up(u, b, p, a, axes) - u[b, p]) - (shift_up(u, a, p, b, axes) - u[a, p])


def curl_adjoint(g, a, p, axes):
    b, c = (a + 1) % 3, (a + 2) % 3
    return (shift_down(g, b, p, c, axes) - g[b, p]) - (shift_down(g, c, p, b, axes) - g[c, p])


def turn(a, by):
    return pltpu.roll(a, by % 8, axis=0) if by % 8 else a


def pack_rows(items):
    packed = []
    for base in range(0, len(items), 8):
        tile = None
        for slot, (a, row) in enumerate(items[base:base + 8]):
            piece = turn(a, slot - row)
            tile = piece if tile is None else jnp.where(sublane(a.shape) == slot, piece, tile)
        packed.append(tile)
    return packed


def with_rows(tile, *items):
    for ref, slot, row in items:
        piece = turn(ref[slot // 8], row - slot % 8)
        tile = piece if tile is None else jnp.where(sublane(piece.shape) == row, piece, tile)
    return tile


def joined(own_part, halo):
    return jnp.concatenate([own_part, halo], axis=0)


def kernel(n_gx, n_gy, r_hbm, fm_hbm, es_hbm, em_hbm, ns_hbm, vel_hbm, ec_hbm,
           r_ref, fm_ref, es_ref, em_ref, ns_ref, vel_ref, ec_ref,
           x_right, x_left, y_upper, y_lower, cr_upper, cr_lower, cl_upper, cl_lower,
           in_left, in_right, in_below, in_above, in_cl_below, in_cl_above, in_cr_below, in_cr_above,
           es_out, es_in, faced, ef_right, ef_left, in_ef_left, in_ef_right,
           e_left, e_right, e_next, e_prev, e_ca, e_cb, in_e_right, in_e_left, in_e_next, in_e_prev, in_e_ca, in_e_cb,
           res_right, res_left, res_upper, res_lower, rr_upper, rr_lower, rl_upper, rl_lower,
           in_res_left, in_res_right, in_res_below, in_res_above, in_rl_below, in_rl_above, in_rr_below, in_rr_above, win, in_win, in_win_right, in_win_left,
           load_sem, send_sem, recv_sem):
    gx, gy = lax.axis_index("gx"), lax.axis_index("gy")

    def at(dx, dy):
        return (lax.rem(gx + dx + n_gx, n_gx), lax.rem(gy + dy + n_gy, n_gy))

    barrier = pltpu.get_barrier_semaphore()
    greeted = [at(a, b) for a in (1, -1) for b in (-1, 0, 1)] + [at(0, j) for j in range(1, n_gy)]
    for peer in greeted:
        pl.semaphore_signal(barrier, inc=1, device_id=peer, device_id_type=MESH)
    loads = [pltpu.make_async_copy(src, dst, load_sem.at[i]) for i, (src, dst) in enumerate(
        ((r_hbm, r_ref), (fm_hbm, fm_ref), (es_hbm, es_ref), (em_hbm, em_ref), (ns_hbm, ns_ref)))]
    for load in loads:
        load.start()
    sent = []

    def message(src, dst, peer):
        index = len(sent)
        copy = pltpu.make_async_remote_copy(
            src_ref=src, dst_ref=dst, send_sem=send_sem.at[index], recv_sem=recv_sem.at[index],
            device_id=peer, device_id_type=MESH)
        sent.append(copy)
        copy.start()
        return copy

    for load in loads[:2]:
        load.wait()
    r = [[r_ref[c, p] for p in range(2)] for c in range(3)]
    fm = [[fm_ref[c, p] for p in range(2)] for c in range(3)]
    s1 = [[damping * r[c][p] / (fm[c][p] + 2.0 * grad_div_weight) for p in range(2)] for c in range(3)]
    known = [s1[0][1] - s1[0][0], up(s1[2][0], 1) - s1[2][0]]
    wide = sublane(known[0].shape)
    partial = known[0] + (jnp.where(wide == 7, 0.0, up(s1[1][0], 0)) - s1[1][0]) + known[1]
    to_right = [r[c][1] for c in range(3)] + [fm[c][1] for c in range(3)] + [partial]
    to_left = [r[0][0], fm[0][0], known[0] + known[1], s1[1][0]]
    cells = [(c, p) for c in range(3) for p in range(2)]
    for ref, parts in (
            (x_right, to_right), (x_left, to_left),
            (y_upper, pack_rows([(f[c][p], 7) for f in (r, fm) for c, p in cells] + [(s1[c][p], 6) for c, p in cells])),
            (y_lower, pack_rows([(f[p], 0) for f in (r[1], fm[1], s1[0], s1[2]) for p in range(2)]
                                + [(s1[1][p], 1) for p in range(2)])),
            (cr_upper, pack_rows([(s1[c][1], 7) for c in range(3)])),
            (cr_lower, pack_rows([(r[1][1], 0), (fm[1][1], 0), (s1[0][1], 0), (s1[2][1], 0), (s1[1][1], 1), (s1[1][0], 0)])),
            (cl_upper, pack_rows([(to_left[i], 7) for i in range(4)] + [(s1[0][0], 6)])),
            (cl_lower, pack_rows([(s1[1][0], 0), (s1[0][0], 0)]))):
        for i, part in enumerate(parts):
            ref[i] = part

    for load in loads[2:]:
        load.wait()
    nz, ny = es_ref.shape[2], es_ref.shape[3]

    def wrapped(field):
        return jnp.concatenate([field, field[:, :16], field[:, ny - 16:]], axis=1)

    es = {(c, p): wrapped(es_ref[c, p]) for c in range(3) for p in range(2)}
    em = {(c, p): wrapped(em_ref[c, p]) for c in range(3) for p in range(2)}
    ns = {p: wrapped(ns_ref[p]) for p in range(2)}
    products = {key: em[key] * es[key] for key in es}
    for i, field in enumerate([products[c, 0] for c in range(3)] + [ns[0]]):
        e_left[i] = field
    e_right[0] = products[0, 1]
    for i, field in enumerate([products[key] for key in cells] + [ns[0], ns[1]]):
        e_next[i] = field[0:8]
    for p in range(2):
        e_prev[p] = products[2, p][nz - 8:]
    e_ca[0] = products[2, 0][nz - 8:]
    e_cb[0] = products[0, 1][0:8]

    order = [(c, p) for p in range(2) for c in range(3)]
    sub = sublane((8, 128))
    halos = []
    for t in range(2):
        group = [es[key] for key in order[4 * t:4 * t + 4]]
        group += [group[0]] * (4 - len(group))
        turned = jnp.concatenate(group, axis=0).T
        es_out[:, t] = turned[:ny].reshape(n_gy, 8, 128)
        after = turned[8:ny + 8].reshape(n_gy, 8, 128)
        before = jnp.concatenate([turned[ny - 8:ny], turned[:ny - 8]], axis=0).reshape(n_gy, 8, 128)
        halos.append((after, before))
    for k in range(n_gy):
        first_halo = jnp.where(sub < 4, halos[0][0][k], halos[0][1][k])
        second_halo = half_turn(jnp.where(sub < 4, halos[1][0][k], halos[1][1][k]))
        es_out[k, 2] = jnp.where((sub == 3) | (sub == 4), second_halo, first_halo)

    pl.semaphore_wait(barrier, len(greeted))

    first = [
        message(cr_upper, in_cl_below, at(1, 1)), message(cr_lower, in_cl_above, at(1, -1)),
        message(cl_upper, in_cr_below, at(-1, 1)), message(cl_lower, in_cr_above, at(-1, -1)),
        message(x_left, in_right, at(-1, 0)), message(x_right, in_left, at(1, 0)),
        message(y_upper, in_below, at(0, 1)), message(y_lower, in_above, at(0, -1)),
    ]
    exchange = []
    for j in [k for k in sorted(range(n_gy), key=lambda j: (abs(j % 4 - 2), -min(j, n_gy - j))) if k]:
        peer = at(0, j)
        exchange.append(message(es_out.at[peer[1]], es_in.at[gy], peer))
    es_in[gy] = es_out[gy]
    edge_halo = [
        message(e_left, in_e_right, at(-1, 0)), message(e_right, in_e_left, at(1, 0)),
        message(e_next, in_e_next, at(0, -1)), message(e_prev, in_e_prev, at(0, 1)),
        message(e_ca, in_e_ca, at(-1, 1)), message(e_cb, in_e_cb, at(1, -1)),
    ]

    for copy in first:
        copy.wait_recv()

    rr, ff, dd, ss = {}, {}, {}, {}
    for i, (c, p) in enumerate(cells):
        above = c == 1
        rr[c, p] = joined(r_ref[c, p], with_rows(None, (in_below, i, 7), *[(in_above, p, 0)] * above))
        ff[c, p] = joined(fm_ref[c, p], with_rows(None, (in_below, 6 + i, 7), *[(in_above, 2 + p, 0)] * above))
    for c in range(3):
        rr[c, -1] = joined(in_left[c], with_rows(None, (in_cl_above, 0, 0)) if c == 1 else in_left[c])
        ff[c, -1] = joined(in_left[3 + c], with_rows(None, (in_cl_above, 1, 0)) if c == 1 else in_left[3 + c])
    rr[0, 2] = joined(in_right[0], with_rows(None, (in_cr_below, 0, 7)))
    ff[0, 2] = joined(in_right[1], with_rows(None, (in_cr_below, 1, 7)))
    for key in rr:
        dd[key] = ff[key] + 2.0 * grad_div_weight
        ss[key] = damping * rr[key] / dd[key]

    def more_rows(key, *items):
        ss[key] = joined(ss[key][0:8], with_rows(ss[key][8:16], *items))

    for i, (c, p) in enumerate(cells):
        more_rows((c, p), (in_below, 12 + i, 6), (in_above, (4, 8, 6)[c] + p, 1 if c == 1 else 0))
    for c in range(3):
        more_rows((c, -1), (in_cl_below, c, 7), (in_cl_above, (2, 4, 3)[c], 1 if c == 1 else 0))
    more_rows((0, 2), (in_cr_below, 4, 6), (in_cr_above, 1, 0))
    known = joined(in_right[2], with_rows(None, (in_cr_below, 2, 7)))
    second_flux = joined(in_right[3], with_rows(None, (in_cr_below, 3, 7), (in_cr_above, 0, 0)))

    def divergence(u, p):
        return (u[0, p + 1] - u[0, p]) + (up(u[1, p], 0) - u[1, p]) + (up(u[2, p], 1) - u[2, p])

    def apply_faces(u, div, c, p):
        shifted = div[p - 1] if c == 0 else down(div[p], c - 1)
        return ff[c, p] * u[c, p] + grad_div_weight * (shifted - div[p])

    div1 = {p: divergence(ss, p) for p in range(-1, 2)}
    div1[2] = known + (up(second_flux, 0) - second_flux)
    far = in_left[6]
    far = jnp.where(wide == 7, far + turn(in_cl_above[0], 2), far)
    div1[-2] = joined(far, far)
    tt = {key: ss[key] + damping * (rr[key] - apply_faces(ss, div1, *key)) / dd[key] for key in rr}
    div2 = {p: divergence(tt, p) for p in range(-1, 2)}
    res = {(c, p): rr[c, p] - apply_faces(tt, div2, c, p) for c in range(3) for p in range(2)}

    mine = {key: res[key][0:8] for key in res}
    for ref, parts in (
            (res_right, [mine[1, 0], mine[2, 0], mine[0, 1], mine[1, 1], mine[2, 1]]),
            (res_left, [mine[0, 0], mine[1, 0], mine[2, 0]]),
            (res_upper, pack_rows([(mine[key], 7) for key in cells] + [(mine[c, p], 6) for c in (0, 2) for p in range(2)])),
            (res_lower, pack_rows([(mine[key], 0) for key in cells])),
            (rr_upper, pack_rows([(mine[c, 1], 7) for c in range(3)])),
            (rr_lower, pack_rows([(mine[c, 1], 0) for c in range(3)] + [(mine[1, 0], 0)])),
            (rl_upper, pack_rows([(mine[c, 0], 7) for c in range(3)] + [(mine[0, 0], 6)])),
            (rl_lower, pack_rows([(mine[c, 0], 0) for c in range(2)]))):
        for i, part in enumerate(parts):
            ref[i] = part
    second = [
        message(rr_upper, in_rl_below, at(1, 1)), message(rr_lower, in_rl_above, at(1, -1)),
        message(rl_upper, in_rr_below, at(-1, 1)), message(rl_lower, in_rr_above, at(-1, -1)),
        message(res_right, in_res_left, at(1, 0)), message(res_left, in_res_right, at(-1, 0)),
        message(res_upper, in_res_below, at(0, 1)), message(res_lower, in_res_above, at(0, -1)),
    ]

    span = nz + 8
    lane = lax.broadcasted_iota(jnp.int32, (8, 128), 1)
    total = r_ref.shape[3]
    for k in range(n_gy):
        for p in range(2):
            tile = None
            for c in range(3):
                shift = (span * c - (nz * k - 4)) % total
                piece = (pltpu.roll(mine[c, p], shift, axis=1) if shift else mine[c, p])[:, :128]
                tile = piece if tile is None else jnp.where(lane >= span * c, piece, tile)
            win[k, p] = tile
    windows = []
    for j in [k for k in sorted(range(n_gy), key=lambda j: (abs(j % 4 - 2), -min(j, n_gy - j))) if k]:
        peer = at(0, j)
        windows.append(message(win.at[peer[1]], in_win.at[gy], peer))
    for j in sorted(range(n_gy), key=lambda j: (abs(j % 4 - 2), -min(j, n_gy - j))):
        for side, p, dst in ((1, 1, in_win_left), (-1, 0, in_win_right)):
            peer = at(side, j)
            windows.append(message(win.at[peer[1], p], dst.at[gy], peer))
    in_win[gy] = win[gy]

    for copy in exchange:
        copy.wait_recv()
    lane4 = lane // nz
    for i, (c, p) in enumerate(order):
        t, q = divmod(i, 4)
        for m in range(total // 128):
            for h in range(2):
                tile = None
                for jj in range(4):
                    piece = es_in[4 * m + jj, 2 if h else t]
                    if jj != q:
                        piece = pltpu.roll(piece, (nz * (jj - q)) % 128, axis=1)
                    tile = piece if tile is None else jnp.where(lane4 == jj, piece, tile)
                faced[p, c, 8 * h:8 * h + 8, 128 * m:128 * m + 128] = half_turn(tile) if h and t else tile
    for ref, p, comps in ((ef_right, 1, (0, 1, 2)), (ef_left, 0, (1, 2))):
        tile = None
        for i, c in enumerate(comps):
            ref[i] = faced[p, c, 0:8]
            piece = faced[p, c, 8:16]
            piece = pltpu.roll(piece, 2 * i, axis=0) if i else piece
            tile = piece if tile is None else jnp.where((wide == 2 * i) | (wide == 2 * i - 1), piece, tile)
        ref[len(comps)] = tile
    scale_halo = [message(ef_right, in_ef_left, at(1, 0)), message(ef_left, in_ef_right, at(-1, 0))]

    for copy in edge_halo:
        copy.wait_recv()
    low = sub < 4
    both = {}
    for i, (c, p) in enumerate(cells):
        halo = in_e_next[i]
        if c == 2:
            halo = jnp.where(low, halo, in_e_prev[p])
        both[c, p] = joined(wrapped(em_ref[c, p]) * wrapped(es_ref[c, p]), halo)
    node = {p: joined(wrapped(ns_ref[p]), in_e_next[6 + p]) for p in range(2)}
    both[0, -1] = joined(in_e_left[0], in_e_cb[0])
    for c in range(3):
        both[c, 2] = joined(in_e_right[c], in_e_ca[0])
    node[2] = joined(in_e_right[3], in_e_ca[0])
    for copy in second + scale_halo:
        copy.wait_recv()

    def ef_halo(ref, count, i):
        tile = ref[count]
        return joined(ref[i], pltpu.roll(tile, 8 - 2 * i, axis=0) if i else tile)

    for i, (c, p) in enumerate(cells):
        rows = [(in_res_below, i, 7), (in_res_above, i, 0)] + [(in_res_below, 6 + c + p, 6)] * (c != 1)
        res[c, p] = joined(mine[c, p], with_rows(None, *rows))
    res[1, -2] = joined(in_res_left[0], with_rows(None, (in_rl_above, 3, 0)))
    res[2, -2] = joined(in_res_left[1], in_res_left[1])
    for c in range(3):
        res[c, -1] = joined(in_res_left[2 + c], with_rows(None, (in_rl_below, c, 7), (in_rl_above, c, 0)))
        rows = [(in_rr_below, c, 7)] + [(in_rr_below, 3, 6)] * (c == 0) + [(in_rr_above, c, 0)] * (c < 2)
        res[c, 2] = joined(in_res_right[c], with_rows(None, *rows))
    scale = {(c, p): faced[p, c] for c in range(3) for p in range(2)}
    for c in range(3):
        scale[c, -1] = ef_halo(in_ef_left, 3, c)
    for c in range(1, 3):
        scale[c, 2] = ef_halo(in_ef_right, 2, c - 1)
    sm = {key: scale[key] * curl_adjoint(res, *key, FACE) for key in scale}
    new = {key: tt[key] + curl(sm, *key, FACE) for key in tt}
    div3 = {p: divergence(new, p) for p in range(-1, 2)}
    for c in range(3):
        for p in range(2):
            key = (c, p)
            out = new[key] + damping * (rr[key] - apply_faces(new, div3, c, p)) / dd[key]
            vel_ref[c, p] = out[0:8]

    store = [pltpu.make_async_copy(vel_ref, vel_hbm, load_sem.at[5]), pltpu.make_async_copy(ec_ref, ec_hbm, load_sem.at[6])]
    store[0].start()
    for copy in windows:
        copy.wait_recv()
    g = {}
    for p, ref in ((-1, in_win_left), (0, None), (1, None), (2, in_win_right)):
        rows = (in_win[:, p] if ref is None else ref[...]).reshape(ny, 128)
        turned = jnp.concatenate([rows, rows[:16], rows[ny - 16:]], axis=0).T
        for c in range(3):
            g[c, p] = pltpu.roll(turned[span * c:span * c + span], span - 4, axis=0)
    edge_residual = {key: curl_adjoint(g, *key, EDGE) for key in both}
    ww = {key: both[key] * edge_residual[key] for key in both}
    pot = {}
    for p in range(3):
        adjoint = ((ww[0, p - 1] - ww[0, p]) + (down(ww[1, p], 1) - ww[1, p])) + (down(ww[2, p], 0) - ww[2, p])
        pot[0, p] = node[p] * -adjoint
    for c in range(3):
        for p in range(2):
            ahead = pot[0, p + 1] if c == 0 else up(pot[0, p], EDGE[c - 1])
            smoothed = wrapped(es_ref[c, p]) * edge_residual[c, p][:nz]
            ec_ref[c, p] = (smoothed + (ahead - pot[0, p])[:nz])[:, :ny]
    store[1].start()
    for copy in sent:
        copy.wait_send()
    for copy in store:
        copy.wait()


def hand_over(a, b, a_out, b_out):
    a_out[...] = a[...]
    b_out[...] = b[...]


def on_device(right_side, face_mass, edge_scale, edge_mass, node_scale):
    n_gx, n_gy = lax.axis_size("gx"), lax.axis_size("gy")
    edge_scale, edge_mass, node_scale = (jnp.swapaxes(a, -1, -2) for a in (edge_scale, edge_mass, node_scale))
    total, nz = right_side.shape[3], edge_scale.shape[2]

    def own(a):
        return pltpu.VMEM(a.shape, jnp.float32)

    def rows(*lead):
        return pltpu.VMEM((*lead, 8, total), jnp.float32)

    def tile(*lead):
        return pltpu.VMEM((*lead, 8, 128), jnp.float32)

    def field(*lead):
        return pltpu.VMEM((*lead, nz, 128), jnp.float32)

    arguments = (right_side, face_mass, edge_scale, edge_mass, node_scale)
    first = [rows(7), rows(4), rows(3), rows(2), rows(1), rows(1), rows(1), rows(1)]
    second = [rows(5), rows(3), rows(2), rows(1), rows(1), rows(1), rows(1), rows(1)]
    halo = [field(4), field(1), tile(8), tile(2), tile(1), tile(1)]
    count = 24 + 5 * n_gy - 2
    velocity, correction = pl.pallas_call(
        functools.partial(kernel, n_gx, n_gy),
        out_shape=(jax.ShapeDtypeStruct(right_side.shape, jnp.float32),
                   jax.ShapeDtypeStruct(edge_scale.shape, jnp.float32)),
        in_specs=[pl.BlockSpec(memory_space=pltpu.HBM)] * 5,
        out_specs=(pl.BlockSpec(memory_space=pl.ANY),) * 2,
        scratch_shapes=[own(a) for a in (*arguments, right_side, edge_scale)] + first + first + [
            tile(n_gy, 3), tile(n_gy, 3), pltpu.VMEM((2, 3, 16, total), jnp.float32),
            rows(4), rows(3), rows(4), rows(3)] + halo + halo + [
            *second, *second, tile(n_gy, 2), tile(n_gy, 2), tile(n_gy), tile(n_gy),
            pltpu.SemaphoreType.DMA((7,)),
            pltpu.SemaphoreType.DMA((count,)), pltpu.SemaphoreType.DMA((count,)),
        ],
        compiler_params=pltpu.CompilerParams(
            collective_id=0, has_side_effects=True, vmem_limit_bytes=60 * 1024 * 1024),
    )(*arguments)
    inside = pl.BlockSpec(memory_space=pltpu.VMEM)
    velocity, correction = pl.pallas_call(
        hand_over,
        out_shape=(jax.ShapeDtypeStruct(velocity.shape, jnp.float32),
                   jax.ShapeDtypeStruct(correction.shape, jnp.float32)),
        in_specs=[inside, inside],
        out_specs=(inside, inside),
        compiler_params=pltpu.CompilerParams(vmem_limit_bytes=60 * 1024 * 1024),
    )(velocity, correction)
    return velocity, jnp.swapaxes(correction, 2, 3)


def solution(mesh):
    placed = (
        P(None, "gx", "gy", None),
        P(None, "gx", "gy", None),
        P(None, "gx", None, "gy"),
        P(None, "gx", None, "gy"),
        P("gx", None, "gy"),
    )
    return jax.shard_map(
        on_device,
        mesh=mesh,
        in_specs=placed,
        out_specs=(P(None, "gx", "gy", None), P(None, "gx", None, "gy")),
        check_vma=False,
    )
```

```python
import functools

import jax
import jax.numpy as jnp
from jax import lax
from jax.experimental import pallas as pl
from jax.experimental.pallas import tpu as pltpu
from jax.sharding import PartitionSpec as P

MESH = pl.DeviceIdType.MESH
grad_div_weight = 1.0
damping = 0.3


def up(a, axis):
    return pltpu.roll(a, a.shape[axis] - 1, axis=axis)


def down(a, axis):
    return pltpu.roll(a, 1, axis=axis)


def half_turn(a):
    return pltpu.roll(a, 4, axis=0)


def sublane(shape):
    return lax.broadcasted_iota(jnp.int32, shape, len(shape) - 2)


def shift_up(u, c, p, direction, axes):
    return u[c, p + 1] if direction == 0 else up(u[c, p], axes[direction - 1])


def shift_down(u, c, p, direction, axes):
    return u[c, p - 1] if direction == 0 else down(u[c, p], axes[direction - 1])


FACE = (0, 1)
EDGE = (1, 0)


def curl(u, c, p, axes):
    a, b = (c + 1) % 3, (c + 2) % 3
    return (shift_up(u, b, p, a, axes) - u[b, p]) - (shift_up(u, a, p, b, axes) - u[a, p])


def curl_adjoint(g, a, p, axes):
    b, c = (a + 1) % 3, (a + 2) % 3
    return (shift_down(g, b, p, c, axes) - g[b, p]) - (shift_down(g, c, p, b, axes) - g[c, p])


def turn(a, by):
    return pltpu.roll(a, by % 8, axis=0) if by % 8 else a


def pack_rows(items):
    packed = []
    for base in range(0, len(items), 8):
        tile = None
        for slot, (a, row) in enumerate(items[base:base + 8]):
            piece = turn(a, slot - row)
            tile = piece if tile is None else jnp.where(sublane(a.shape) == slot, piece, tile)
        packed.append(tile)
    return packed


def with_rows(tile, *items):
    for ref, slot, row in items:
        piece = turn(ref[slot // 8], row - slot % 8)
        tile = piece if tile is None else jnp.where(sublane(piece.shape) == row, piece, tile)
    return tile


def joined(own_part, halo):
    return jnp.concatenate([own_part, halo], axis=0)


def kernel(n_gx, n_gy, r_hbm, fm_hbm, es_hbm, em_hbm, ns_hbm, vel_hbm, ec_hbm,
           r_ref, fm_ref, es_ref, em_ref, ns_ref, vel_ref, ec_ref,
           x_right, x_left, y_upper, y_lower, cr_upper, cr_lower, cl_upper, cl_lower,
           in_left, in_right, in_below, in_above, in_cl_below, in_cl_above, in_cr_below, in_cr_above,
           es_out, es_in, faced, ef_right, ef_left, in_ef_left, in_ef_right,
           e_left, e_right, e_next, e_prev, e_ca, e_cb, in_e_right, in_e_left, in_e_next, in_e_prev, in_e_ca, in_e_cb,
           res_right, res_left, res_upper, res_lower, rr_upper, rr_lower, rl_upper, rl_lower,
           in_res_left, in_res_right, in_res_below, in_res_above, in_rl_below, in_rl_above, in_rr_below, in_rr_above, win, in_win, in_win_right, in_win_left,
           load_sem, send_sem, recv_sem):
    gx, gy = lax.axis_index("gx"), lax.axis_index("gy")

    def at(dx, dy):
        return (lax.rem(gx + dx + n_gx, n_gx), lax.rem(gy + dy + n_gy, n_gy))

    barrier = pltpu.get_barrier_semaphore()
    greeted = [at(a, b) for a in (1, -1) for b in (-1, 0, 1)] + [at(0, j) for j in range(1, n_gy)]
    for peer in greeted:
        pl.semaphore_signal(barrier, inc=1, device_id=peer, device_id_type=MESH)
    loads = [pltpu.make_async_copy(src, dst, load_sem.at[i]) for i, (src, dst) in enumerate(
        ((r_hbm, r_ref), (fm_hbm, fm_ref), (es_hbm, es_ref), (em_hbm, em_ref), (ns_hbm, ns_ref)))]
    for load in loads:
        load.start()
    sent = []

    def message(src, dst, peer):
        index = len(sent)
        copy = pltpu.make_async_remote_copy(
            src_ref=src, dst_ref=dst, send_sem=send_sem.at[index], recv_sem=recv_sem.at[index],
            device_id=peer, device_id_type=MESH)
        sent.append(copy)
        copy.start()
        return copy

    for load in loads[:2]:
        load.wait()
    r = [[r_ref[c, p] for p in range(2)] for c in range(3)]
    fm = [[fm_ref[c, p] for p in range(2)] for c in range(3)]
    s1 = [[damping * r[c][p] / (fm[c][p] + 2.0 * grad_div_weight) for p in range(2)] for c in range(3)]
    known = [s1[0][1] - s1[0][0], up(s1[2][0], 1) - s1[2][0]]
    wide = sublane(known[0].shape)
    partial = known[0] + (jnp.where(wide == 7, 0.0, up(s1[1][0], 0)) - s1[1][0]) + known[1]
    to_right = [r[c][1] for c in range(3)] + [fm[c][1] for c in range(3)] + [partial]
    to_left = [r[0][0], fm[0][0], known[0] + known[1], s1[1][0]]
    cells = [(c, p) for c in range(3) for p in range(2)]
    for ref, parts in (
            (x_right, to_right), (x_left, to_left),
            (y_upper, pack_rows([(f[c][p], 7) for f in (r, fm) for c, p in cells] + [(s1[c][p], 6) for c, p in cells])),
            (y_lower, pack_rows([(f[p], 0) for f in (r[1], fm[1], s1[0], s1[2]) for p in range(2)]
                                + [(s1[1][p], 1) for p in range(2)])),
            (cr_upper, pack_rows([(s1[c][1], 7) for c in range(3)])),
            (cr_lower, pack_rows([(r[1][1], 0), (fm[1][1], 0), (s1[0][1], 0), (s1[2][1], 0), (s1[1][1], 1), (s1[1][0], 0)])),
            (cl_upper, pack_rows([(to_left[i], 7) for i in range(4)] + [(s1[0][0], 6)])),
            (cl_lower, pack_rows([(s1[1][0], 0), (s1[0][0], 0)]))):
        for i, part in enumerate(parts):
            ref[i] = part

    for load in loads[2:]:
        load.wait()
    nz, ny = es_ref.shape[2], es_ref.shape[3]

    def wrapped(field):
        return jnp.concatenate([field, field[:, :16], field[:, ny - 16:]], axis=1)

    es = {(c, p): wrapped(es_ref[c, p]) for c in range(3) for p in range(2)}
    em = {(c, p): wrapped(em_ref[c, p]) for c in range(3) for p in range(2)}
    ns = {p: wrapped(ns_ref[p]) for p in range(2)}
    products = {key: em[key] * es[key] for key in es}
    for i, field in enumerate([products[c, 0] for c in range(3)] + [ns[0]]):
        e_left[i] = field
    e_right[0] = products[0, 1]
    for i, field in enumerate([products[key] for key in cells] + [ns[0], ns[1]]):
        e_next[i] = field[0:8]
    for p in range(2):
        e_prev[p] = products[2, p][nz - 8:]
    e_ca[0] = products[2, 0][nz - 8:]
    e_cb[0] = products[0, 1][0:8]

    order = [(c, p) for p in range(2) for c in range(3)]
    sub = sublane((8, 128))
    halos = []
    for t in range(2):
        group = [es[key] for key in order[4 * t:4 * t + 4]]
        group += [group[0]] * (4 - len(group))
        turned = jnp.concatenate(group, axis=0).T
        es_out[:, t] = turned[:ny].reshape(n_gy, 8, 128)
        after = turned[8:ny + 8].reshape(n_gy, 8, 128)
        before = jnp.concatenate([turned[ny - 8:ny], turned[:ny - 8]], axis=0).reshape(n_gy, 8, 128)
        halos.append((after, before))
    for k in range(n_gy):
        first_halo = jnp.where(sub < 4, halos[0][0][k], halos[0][1][k])
        second_halo = half_turn(jnp.where(sub < 4, halos[1][0][k], halos[1][1][k]))
        es_out[k, 2] = jnp.where((sub == 3) | (sub == 4), second_halo, first_halo)

    pl.semaphore_wait(barrier, len(greeted))

    first = [
        message(cr_upper, in_cl_below, at(1, 1)), message(cr_lower, in_cl_above, at(1, -1)),
        message(cl_upper, in_cr_below, at(-1, 1)), message(cl_lower, in_cr_above, at(-1, -1)),
        message(x_left, in_right, at(-1, 0)), message(x_right, in_left, at(1, 0)),
        message(y_upper, in_below, at(0, 1)), message(y_lower, in_above, at(0, -1)),
    ]
    exchange = []
    for j in [k for k in sorted(range(n_gy), key=lambda j: (abs(j % 4 - 2), -min(j, n_gy - j))) if k]:
        peer = at(0, j)
        exchange.append(message(es_out.at[peer[1]], es_in.at[gy], peer))
    es_in[gy] = es_out[gy]
    edge_halo = [
        message(e_left, in_e_right, at(-1, 0)), message(e_right, in_e_left, at(1, 0)),
        message(e_next, in_e_next, at(0, -1)), message(e_prev, in_e_prev, at(0, 1)),
        message(e_ca, in_e_ca, at(-1, 1)), message(e_cb, in_e_cb, at(1, -1)),
    ]

    for copy in first:
        copy.wait_recv()

    rr, ff, dd, ss = {}, {}, {}, {}
    for i, (c, p) in enumerate(cells):
        above = c == 1
        rr[c, p] = joined(r_ref[c, p], with_rows(None, (in_below, i, 7), *[(in_above, p, 0)] * above))
        ff[c, p] = joined(fm_ref[c, p], with_rows(None, (in_below, 6 + i, 7), *[(in_above, 2 + p, 0)] * above))
    for c in range(3):
        rr[c, -1] = joined(in_left[c], with_rows(None, (in_cl_above, 0, 0)) if c == 1 else in_left[c])
        ff[c, -1] = joined(in_left[3 + c], with_rows(None, (in_cl_above, 1, 0)) if c == 1 else in_left[3 + c])
    rr[0, 2] = joined(in_right[0], with_rows(None, (in_cr_below, 0, 7)))
    ff[0, 2] = joined(in_right[1], with_rows(None, (in_cr_below, 1, 7)))
    for key in rr:
        dd[key] = ff[key] + 2.0 * grad_div_weight
        ss[key] = damping * rr[key] / dd[key]

    def more_rows(key, *items):
        ss[key] = joined(ss[key][0:8], with_rows(ss[key][8:16], *items))

    for i, (c, p) in enumerate(cells):
        more_rows((c, p), (in_below, 12 + i, 6), (in_above, (4, 8, 6)[c] + p, 1 if c == 1 else 0))
    for c in range(3):
        more_rows((c, -1), (in_cl_below, c, 7), (in_cl_above, (2, 4, 3)[c], 1 if c == 1 else 0))
    more_rows((0, 2), (in_cr_below, 4, 6), (in_cr_above, 1, 0))
    known = joined(in_right[2], with_rows(None, (in_cr_below, 2, 7)))
    second_flux = joined(in_right[3], with_rows(None, (in_cr_below, 3, 7), (in_cr_above, 0, 0)))

    def divergence(u, p):
        return (u[0, p + 1] - u[0, p]) + (up(u[1, p], 0) - u[1, p]) + (up(u[2, p], 1) - u[2, p])

    def apply_faces(u, div, c, p):
        shifted = div[p - 1] if c == 0 else down(div[p], c - 1)
        return ff[c, p] * u[c, p] + grad_div_weight * (shifted - div[p])

    div1 = {p: divergence(ss, p) for p in range(-1, 2)}
    div1[2] = known + (up(second_flux, 0) - second_flux)
    far = in_left[6]
    far = jnp.where(wide == 7, far + turn(in_cl_above[0], 2), far)
    div1[-2] = joined(far, far)
    tt = {key: ss[key] + damping * (rr[key] - apply_faces(ss, div1, *key)) / dd[key] for key in rr}
    div2 = {p: divergence(tt, p) for p in range(-1, 2)}
    res = {(c, p): rr[c, p] - apply_faces(tt, div2, c, p) for c in range(3) for p in range(2)}

    mine = {key: res[key][0:8] for key in res}
    span = nz + 8
    lane = lax.broadcasted_iota(jnp.int32, (8, 128), 1)
    total = r_ref.shape[3]
    for k in range(n_gy):
        for p in range(2):
            tile = None
            for c in range(3):
                shift = (span * c - (nz * k - 4)) % total
                piece = (pltpu.roll(mine[c, p], shift, axis=1) if shift else mine[c, p])[:, :128]
                tile = piece if tile is None else jnp.where(lane >= span * c, piece, tile)
            win[k, p] = tile
    windows = []
    for j in [k for k in sorted(range(n_gy), key=lambda j: (abs(j % 4 - 2), -min(j, n_gy - j))) if k]:
        peer = at(0, j)
        windows.append(message(win.at[peer[1]], in_win.at[gy], peer))
    in_win[gy] = win[gy]

    for ref, parts in (
            (res_right, [mine[1, 0], mine[2, 0], mine[0, 1], mine[1, 1], mine[2, 1]]),
            (res_left, [mine[0, 0], mine[1, 0], mine[2, 0]]),
            (res_upper, pack_rows([(mine[key], 7) for key in cells] + [(mine[c, p], 6) for c in (0, 2) for p in range(2)])),
            (res_lower, pack_rows([(mine[key], 0) for key in cells])),
            (rr_upper, pack_rows([(mine[c, 1], 7) for c in range(3)])),
            (rr_lower, pack_rows([(mine[c, 1], 0) for c in range(3)] + [(mine[1, 0], 0)])),
            (rl_upper, pack_rows([(mine[c, 0], 7) for c in range(3)] + [(mine[0, 0], 6)])),
            (rl_lower, pack_rows([(mine[c, 0], 0) for c in range(2)]))):
        for i, part in enumerate(parts):
            ref[i] = part
    second = [
        message(rr_upper, in_rl_below, at(1, 1)), message(rr_lower, in_rl_above, at(1, -1)),
        message(rl_upper, in_rr_below, at(-1, 1)), message(rl_lower, in_rr_above, at(-1, -1)),
        message(res_right, in_res_left, at(1, 0)), message(res_left, in_res_right, at(-1, 0)),
        message(res_upper, in_res_below, at(0, 1)), message(res_lower, in_res_above, at(0, -1)),
    ]


    for copy in exchange:
        copy.wait_recv()
    lane4 = lane // nz
    for i, (c, p) in enumerate(order):
        t, q = divmod(i, 4)
        for m in range(total // 128):
            for h in range(2):
                tile = None
                for jj in range(4):
                    piece = es_in[4 * m + jj, 2 if h else t]
                    if jj != q:
                        piece = pltpu.roll(piece, (nz * (jj - q)) % 128, axis=1)
                    tile = piece if tile is None else jnp.where(lane4 == jj, piece, tile)
                faced[p, c, 8 * h:8 * h + 8, 128 * m:128 * m + 128] = half_turn(tile) if h and t else tile
    for ref, p, comps in ((ef_right, 1, (0, 1, 2)), (ef_left, 0, (1, 2))):
        tile = None
        for i, c in enumerate(comps):
            ref[i] = faced[p, c, 0:8]
            piece = faced[p, c, 8:16]
            piece = pltpu.roll(piece, 2 * i, axis=0) if i else piece
            tile = piece if tile is None else jnp.where((wide == 2 * i) | (wide == 2 * i - 1), piece, tile)
        ref[len(comps)] = tile
    scale_halo = [message(ef_right, in_ef_left, at(1, 0)), message(ef_left, in_ef_right, at(-1, 0))]

    for copy in windows + edge_halo:
        copy.wait_recv()
    passed_on = [message(in_win.at[:, 1], in_win_left, at(1, 0)), message(in_win.at[:, 0], in_win_right, at(-1, 0))]
    low = sub < 4
    both = {}
    for i, (c, p) in enumerate(cells):
        halo = in_e_next[i]
        if c == 2:
            halo = jnp.where(low, halo, in_e_prev[p])
        both[c, p] = joined(wrapped(em_ref[c, p]) * wrapped(es_ref[c, p]), halo)
    node = {p: joined(wrapped(ns_ref[p]), in_e_next[6 + p]) for p in range(2)}
    both[0, -1] = joined(in_e_left[0], in_e_cb[0])
    for c in range(3):
        both[c, 2] = joined(in_e_right[c], in_e_ca[0])
    node[2] = joined(in_e_right[3], in_e_ca[0])
    for copy in second + scale_halo:
        copy.wait_recv()

    def ef_halo(ref, count, i):
        tile = ref[count]
        return joined(ref[i], pltpu.roll(tile, 8 - 2 * i, axis=0) if i else tile)

    for i, (c, p) in enumerate(cells):
        rows = [(in_res_below, i, 7), (in_res_above, i, 0)] + [(in_res_below, 6 + c + p, 6)] * (c != 1)
        res[c, p] = joined(mine[c, p], with_rows(None, *rows))
    res[1, -2] = joined(in_res_left[0], with_rows(None, (in_rl_above, 3, 0)))
    res[2, -2] = joined(in_res_left[1], in_res_left[1])
    for c in range(3):
        res[c, -1] = joined(in_res_left[2 + c], with_rows(None, (in_rl_below, c, 7), (in_rl_above, c, 0)))
        rows = [(in_rr_below, c, 7)] + [(in_rr_below, 3, 6)] * (c == 0) + [(in_rr_above, c, 0)] * (c < 2)
        res[c, 2] = joined(in_res_right[c], with_rows(None, *rows))
    scale = {(c, p): faced[p, c] for c in range(3) for p in range(2)}
    for c in range(3):
        scale[c, -1] = ef_halo(in_ef_left, 3, c)
    for c in range(1, 3):
        scale[c, 2] = ef_halo(in_ef_right, 2, c - 1)
    sm = {key: scale[key] * curl_adjoint(res, *key, FACE) for key in scale}
    new = {key: tt[key] + curl(sm, *key, FACE) for key in tt}
    div3 = {p: divergence(new, p) for p in range(-1, 2)}
    for c in range(3):
        for p in range(2):
            key = (c, p)
            out = new[key] + damping * (rr[key] - apply_faces(new, div3, c, p)) / dd[key]
            vel_ref[c, p] = out[0:8]

    store = [pltpu.make_async_copy(vel_ref, vel_hbm, load_sem.at[5]), pltpu.make_async_copy(ec_ref, ec_hbm, load_sem.at[6])]
    store[0].start()
    for copy in passed_on:
        copy.wait_recv()
    g = {}
    for p, ref in ((-1, in_win_left), (0, None), (1, None), (2, in_win_right)):
        rows = (in_win[:, p] if ref is None else ref[...]).reshape(ny, 128)
        turned = jnp.concatenate([rows, rows[:16], rows[ny - 16:]], axis=0).T
        for c in range(3):
            g[c, p] = pltpu.roll(turned[span * c:span * c + span], span - 4, axis=0)
    edge_residual = {key: curl_adjoint(g, *key, EDGE) for key in both}
    ww = {key: both[key] * edge_residual[key] for key in both}
    pot = {}
    for p in range(3):
        adjoint = ((ww[0, p - 1] - ww[0, p]) + (down(ww[1, p], 1) - ww[1, p])) + (down(ww[2, p], 0) - ww[2, p])
        pot[0, p] = node[p] * -adjoint
    for c in range(3):
        for p in range(2):
            ahead = pot[0, p + 1] if c == 0 else up(pot[0, p], EDGE[c - 1])
            smoothed = wrapped(es_ref[c, p]) * edge_residual[c, p][:nz]
            ec_ref[c, p] = (smoothed + (ahead - pot[0, p])[:nz])[:, :ny]
    store[1].start()
    for copy in sent:
        copy.wait_send()
    for copy in store:
        copy.wait()


def hand_over(a, b, a_out, b_out):
    a_out[...] = a[...]
    b_out[...] = b[...]


def on_device(right_side, face_mass, edge_scale, edge_mass, node_scale):
    n_gx, n_gy = lax.axis_size("gx"), lax.axis_size("gy")
    edge_scale, edge_mass, node_scale = (jnp.swapaxes(a, -1, -2) for a in (edge_scale, edge_mass, node_scale))
    total, nz = right_side.shape[3], edge_scale.shape[2]

    def own(a):
        return pltpu.VMEM(a.shape, jnp.float32)

    def rows(*lead):
        return pltpu.VMEM((*lead, 8, total), jnp.float32)

    def tile(*lead):
        return pltpu.VMEM((*lead, 8, 128), jnp.float32)

    def field(*lead):
        return pltpu.VMEM((*lead, nz, 128), jnp.float32)

    arguments = (right_side, face_mass, edge_scale, edge_mass, node_scale)
    first = [rows(7), rows(4), rows(3), rows(2), rows(1), rows(1), rows(1), rows(1)]
    second = [rows(5), rows(3), rows(2), rows(1), rows(1), rows(1), rows(1), rows(1)]
    halo = [field(4), field(1), tile(8), tile(2), tile(1), tile(1)]
    count = 24 + 5 * n_gy - 2
    velocity, correction = pl.pallas_call(
        functools.partial(kernel, n_gx, n_gy),
        out_shape=(jax.ShapeDtypeStruct(right_side.shape, jnp.float32),
                   jax.ShapeDtypeStruct(edge_scale.shape, jnp.float32)),
        in_specs=[pl.BlockSpec(memory_space=pltpu.HBM)] * 5,
        out_specs=(pl.BlockSpec(memory_space=pl.ANY),) * 2,
        scratch_shapes=[own(a) for a in (*arguments, right_side, edge_scale)] + first + first + [
            tile(n_gy, 3), tile(n_gy, 3), pltpu.VMEM((2, 3, 16, total), jnp.float32),
            rows(4), rows(3), rows(4), rows(3)] + halo + halo + [
            *second, *second, tile(n_gy, 2), tile(n_gy, 2), tile(n_gy), tile(n_gy),
            pltpu.SemaphoreType.DMA((7,)),
            pltpu.SemaphoreType.DMA((count,)), pltpu.SemaphoreType.DMA((count,)),
        ],
        compiler_params=pltpu.CompilerParams(
            collective_id=0, has_side_effects=True, vmem_limit_bytes=60 * 1024 * 1024),
    )(*arguments)
    inside = pl.BlockSpec(memory_space=pltpu.VMEM)
    velocity, correction = pl.pallas_call(
        hand_over,
        out_shape=(jax.ShapeDtypeStruct(velocity.shape, jnp.float32),
                   jax.ShapeDtypeStruct(correction.shape, jnp.float32)),
        in_specs=[inside, inside],
        out_specs=(inside, inside),
        compiler_params=pltpu.CompilerParams(vmem_limit_bytes=60 * 1024 * 1024),
    )(velocity, correction)
    return velocity, jnp.swapaxes(correction, 2, 3)


def solution(mesh):
    placed = (
        P(None, "gx", "gy", None),
        P(None, "gx", "gy", None),
        P(None, "gx", None, "gy"),
        P(None, "gx", None, "gy"),
        P("gx", None, "gy"),
    )
    return jax.shard_map(
        on_device,
        mesh=mesh,
        in_specs=placed,
        out_specs=(P(None, "gx", "gy", None), P(None, "gx", None, "gy")),
        check_vma=False,
    )
```

```python
import functools

import jax
import jax.numpy as jnp
from jax import lax
from jax.experimental import pallas as pl
from jax.experimental.pallas import tpu as pltpu
from jax.sharding import PartitionSpec as P

MESH = pl.DeviceIdType.MESH
grad_div_weight = 1.0
damping = 0.3


def up(a, axis):
    return pltpu.roll(a, a.shape[axis] - 1, axis=axis)


def down(a, axis):
    return pltpu.roll(a, 1, axis=axis)


def half_turn(a):
    return pltpu.roll(a, 4, axis=0)


def sublane(shape):
    return lax.broadcasted_iota(jnp.int32, shape, len(shape) - 2)


def shift_up(u, c, p, direction, axes):
    return u[c, p + 1] if direction == 0 else up(u[c, p], axes[direction - 1])


def shift_down(u, c, p, direction, axes):
    return u[c, p - 1] if direction == 0 else down(u[c, p], axes[direction - 1])


FACE = (0, 1)
EDGE = (1, 0)


def curl(u, c, p, axes):
    a, b = (c + 1) % 3, (c + 2) % 3
    return (shift_up(u, b, p, a, axes) - u[b, p]) - (shift_up(u, a, p, b, axes) - u[a, p])


def curl_adjoint(g, a, p, axes):
    b, c = (a + 1) % 3, (a + 2) % 3
    return (shift_down(g, b, p, c, axes) - g[b, p]) - (shift_down(g, c, p, b, axes) - g[c, p])


def turn(a, by):
    return pltpu.roll(a, by % 8, axis=0) if by % 8 else a


def pack_rows(items):
    packed = []
    for base in range(0, len(items), 8):
        tile = None
        for slot, (a, row) in enumerate(items[base:base + 8]):
            piece = turn(a, slot - row)
            tile = piece if tile is None else jnp.where(sublane(a.shape) == slot, piece, tile)
        packed.append(tile)
    return packed


def with_rows(tile, *items):
    for ref, slot, row in items:
        piece = turn(ref[slot // 8], row - slot % 8)
        tile = piece if tile is None else jnp.where(sublane(piece.shape) == row, piece, tile)
    return tile


def joined(own_part, halo):
    return jnp.concatenate([own_part, halo], axis=0)


def kernel(n_gx, n_gy, r_hbm, fm_hbm, es_hbm, em_hbm, ns_hbm, vel_hbm, ec_hbm,
           r_ref, fm_ref, es_ref, em_ref, ns_ref, vel_ref, ec_ref,
           x_right, x_left, y_upper, y_lower, cr_upper, cr_lower, cl_upper, cl_lower,
           in_left, in_right, in_below, in_above, in_cl_below, in_cl_above, in_cr_below, in_cr_above,
           es_out, es_in, faced, ef_right, ef_left, in_ef_left, in_ef_right,
           e_left, e_right, e_next, e_prev, e_ca, e_cb, in_e_right, in_e_left, in_e_next, in_e_prev, in_e_ca, in_e_cb,
           res_right, res_left, res_upper, res_lower, rr_upper, rr_lower, rl_upper, rl_lower,
           in_res_left, in_res_right, in_res_below, in_res_above, in_rl_below, in_rl_above, in_rr_below, in_rr_above, win, in_win, in_win_right, in_win_left,
           load_sem, send_sem, recv_sem):
    gx, gy = lax.axis_index("gx"), lax.axis_index("gy")

    def at(dx, dy):
        return (lax.rem(gx + dx + n_gx, n_gx), lax.rem(gy + dy + n_gy, n_gy))

    barrier = pltpu.get_barrier_semaphore()
    greeted = [at(a, b) for a in (1, -1) for b in (-1, 0, 1)] + [at(0, j) for j in range(1, n_gy)]
    for peer in greeted:
        pl.semaphore_signal(barrier, inc=1, device_id=peer, device_id_type=MESH)
    loads = [pltpu.make_async_copy(src, dst, load_sem.at[i]) for i, (src, dst) in enumerate(
        ((r_hbm, r_ref), (fm_hbm, fm_ref), (es_hbm, es_ref), (em_hbm, em_ref), (ns_hbm, ns_ref)))]
    for load in loads:
        load.start()
    sent = []

    def message(src, dst, peer):
        index = len(sent)
        copy = pltpu.make_async_remote_copy(
            src_ref=src, dst_ref=dst, send_sem=send_sem.at[index], recv_sem=recv_sem.at[index],
            device_id=peer, device_id_type=MESH)
        sent.append(copy)
        copy.start()
        return copy

    for load in loads[:2]:
        load.wait()
    r = [[r_ref[c, p] for p in range(2)] for c in range(3)]
    fm = [[fm_ref[c, p] for p in range(2)] for c in range(3)]
    s1 = [[damping * r[c][p] / (fm[c][p] + 2.0 * grad_div_weight) for p in range(2)] for c in range(3)]
    known = [s1[0][1] - s1[0][0], up(s1[2][0], 1) - s1[2][0]]
    wide = sublane(known[0].shape)
    partial = known[0] + (jnp.where(wide == 7, 0.0, up(s1[1][0], 0)) - s1[1][0]) + known[1]
    to_right = [r[c][1] for c in range(3)] + [fm[c][1] for c in range(3)] + [partial]
    to_left = [r[0][0], fm[0][0], known[0] + known[1], s1[1][0]]
    cells = [(c, p) for c in range(3) for p in range(2)]
    for ref, parts in (
            (x_right, to_right), (x_left, to_left),
            (y_upper, pack_rows([(f[c][p], 7) for f in (r, fm) for c, p in cells] + [(s1[c][p], 6) for c, p in cells])),
            (y_lower, pack_rows([(f[p], 0) for f in (r[1], fm[1], s1[0], s1[2]) for p in range(2)]
                                + [(s1[1][p], 1) for p in range(2)])),
            (cr_upper, pack_rows([(s1[c][1], 7) for c in range(3)])),
            (cr_lower, pack_rows([(r[1][1], 0), (fm[1][1], 0), (s1[0][1], 0), (s1[2][1], 0), (s1[1][1], 1), (s1[1][0], 0)])),
            (cl_upper, pack_rows([(to_left[i], 7) for i in range(4)] + [(s1[0][0], 6)])),
            (cl_lower, pack_rows([(s1[1][0], 0), (s1[0][0], 0)]))):
        for i, part in enumerate(parts):
            ref[i] = part

    for load in loads[2:]:
        load.wait()
    nz, ny = es_ref.shape[2], es_ref.shape[3]

    def wrapped(field):
        return jnp.concatenate([field, field[:, :16], field[:, ny - 16:]], axis=1)

    es = {(c, p): wrapped(es_ref[c, p]) for c in range(3) for p in range(2)}
    em = {(c, p): wrapped(em_ref[c, p]) for c in range(3) for p in range(2)}
    ns = {p: wrapped(ns_ref[p]) for p in range(2)}
    products = {key: em[key] * es[key] for key in es}
    for i, field in enumerate([products[c, 0] for c in range(3)] + [ns[0]]):
        e_left[i] = field
    e_right[0] = products[0, 1]
    e_next[0] = pack_rows([(field[0:8], 0) for field in [products[key] for key in cells] + [ns[0], ns[1]]])[0]
    e_prev[0] = pack_rows([(products[2, p][nz - 8:], 7) for p in range(2)])[0]
    e_ca[0] = products[2, 0][nz - 8:]
    e_cb[0] = products[0, 1][0:8]

    order = [(c, p) for p in range(2) for c in range(3)]
    sub = sublane((8, 128))
    halos = []
    for t in range(2):
        group = [es[key] for key in order[4 * t:4 * t + 4]]
        group += [group[0]] * (4 - len(group))
        turned = jnp.concatenate(group, axis=0).T
        es_out[:, t] = turned[:ny].reshape(n_gy, 8, 128)
        after = turned[8:ny + 8].reshape(n_gy, 8, 128)
        before = jnp.concatenate([turned[ny - 8:ny], turned[:ny - 8]], axis=0).reshape(n_gy, 8, 128)
        halos.append((after, before))
    column = lax.broadcasted_iota(jnp.int32, (8, 128), 1)
    for k in range(n_gy):
        upper = jnp.where(sub < 4, halos[0][0][k], halos[0][1][k])
        lower = jnp.where(sub < 4, halos[1][0][k], halos[1][1][k])
        spare = jnp.where((sub == 1) | (sub == 2), turn(upper, 2), pltpu.roll(upper, 2 * nz, axis=1))
        spare = jnp.where((sub == 3) | (sub == 4), half_turn(pltpu.roll(lower, 2 * nz, axis=1)), spare)
        es_out[k, 1] = jnp.where(column < 2 * nz, es_out[k, 1], spare)

    pl.semaphore_wait(barrier, len(greeted))

    first = [
        message(cr_upper, in_cl_below, at(1, 1)), message(cr_lower, in_cl_above, at(1, -1)),
        message(cl_upper, in_cr_below, at(-1, 1)), message(cl_lower, in_cr_above, at(-1, -1)),
        message(x_left, in_right, at(-1, 0)), message(x_right, in_left, at(1, 0)),
        message(y_upper, in_below, at(0, 1)), message(y_lower, in_above, at(0, -1)),
    ]
    exchange = []
    for j in [k for k in sorted(range(n_gy), key=lambda j: (abs(j % 4 - 2), -min(j, n_gy - j))) if k]:
        peer = at(0, j)
        exchange.append(message(es_out.at[peer[1]], es_in.at[gy], peer))
    es_in[gy] = es_out[gy]
    edge_halo = [
        message(e_left, in_e_right, at(-1, 0)), message(e_right, in_e_left, at(1, 0)),
        message(e_next, in_e_next, at(0, -1)), message(e_prev, in_e_prev, at(0, 1)),
        message(e_ca, in_e_ca, at(-1, 1)), message(e_cb, in_e_cb, at(1, -1)),
    ]

    for copy in exchange:
        copy.wait_recv()
    lane4 = lax.broadcasted_iota(jnp.int32, (8, 128), 1) // nz
    total = r_ref.shape[3]
    for i, (c, p) in enumerate(order):
        t, q = divmod(i, 4)
        for m in range(total // 128):
            for h in range(2):
                tile = None
                for jj in range(4):
                    piece = es_in[4 * m + jj, 1 if h else t]
                    place = 2 + i % 2 if h else q
                    if jj != place:
                        piece = pltpu.roll(piece, (nz * (jj - place)) % 128, axis=1)
                    tile = piece if tile is None else jnp.where(lane4 == jj, piece, tile)
                faced[p, c, 8 * h:8 * h + 8, 128 * m:128 * m + 128] = turn(tile, -2 * (i // 2)) if h else tile
    for ref, p, comps in ((ef_right, 1, (0, 1, 2)), (ef_left, 0, (1, 2))):
        tile = None
        for i, c in enumerate(comps):
            ref[i] = faced[p, c, 0:8]
            piece = faced[p, c, 8:16]
            piece = pltpu.roll(piece, 2 * i, axis=0) if i else piece
            tile = piece if tile is None else jnp.where((wide == 2 * i) | (wide == 2 * i - 1), piece, tile)
        ref[len(comps)] = tile
    scale_halo = [message(ef_right, in_ef_left, at(1, 0)), message(ef_left, in_ef_right, at(-1, 0))]

    for copy in first:
        copy.wait_recv()

    rr, ff, dd, ss = {}, {}, {}, {}
    for i, (c, p) in enumerate(cells):
        above = c == 1
        rr[c, p] = joined(r_ref[c, p], with_rows(None, (in_below, i, 7), *[(in_above, p, 0)] * above))
        ff[c, p] = joined(fm_ref[c, p], with_rows(None, (in_below, 6 + i, 7), *[(in_above, 2 + p, 0)] * above))
    for c in range(3):
        rr[c, -1] = joined(in_left[c], with_rows(None, (in_cl_above, 0, 0)) if c == 1 else in_left[c])
        ff[c, -1] = joined(in_left[3 + c], with_rows(None, (in_cl_above, 1, 0)) if c == 1 else in_left[3 + c])
    rr[0, 2] = joined(in_right[0], with_rows(None, (in_cr_below, 0, 7)))
    ff[0, 2] = joined(in_right[1], with_rows(None, (in_cr_below, 1, 7)))
    for key in rr:
        dd[key] = ff[key] + 2.0 * grad_div_weight
        ss[key] = damping * rr[key] / dd[key]

    def more_rows(key, *items):
        ss[key] = joined(ss[key][0:8], with_rows(ss[key][8:16], *items))

    for i, (c, p) in enumerate(cells):
        more_rows((c, p), (in_below, 12 + i, 6), (in_above, (4, 8, 6)[c] + p, 1 if c == 1 else 0))
    for c in range(3):
        more_rows((c, -1), (in_cl_below, c, 7), (in_cl_above, (2, 4, 3)[c], 1 if c == 1 else 0))
    more_rows((0, 2), (in_cr_below, 4, 6), (in_cr_above, 1, 0))
    known = joined(in_right[2], with_rows(None, (in_cr_below, 2, 7)))
    second_flux = joined(in_right[3], with_rows(None, (in_cr_below, 3, 7), (in_cr_above, 0, 0)))

    def divergence(u, p):
        return (u[0, p + 1] - u[0, p]) + (up(u[1, p], 0) - u[1, p]) + (up(u[2, p], 1) - u[2, p])

    def apply_faces(u, div, c, p):
        shifted = div[p - 1] if c == 0 else down(div[p], c - 1)
        return ff[c, p] * u[c, p] + grad_div_weight * (shifted - div[p])

    div1 = {p: divergence(ss, p) for p in range(-1, 2)}
    div1[2] = known + (up(second_flux, 0) - second_flux)
    far = in_left[6]
    far = jnp.where(wide == 7, far + turn(in_cl_above[0], 2), far)
    div1[-2] = joined(far, far)
    tt = {key: ss[key] + damping * (rr[key] - apply_faces(ss, div1, *key)) / dd[key] for key in rr}
    div2 = {p: divergence(tt, p) for p in range(-1, 2)}
    res = {(c, p): rr[c, p] - apply_faces(tt, div2, c, p) for c in range(3) for p in range(2)}

    mine = {key: res[key][0:8] for key in res}
    span = nz + 8
    lane = lax.broadcasted_iota(jnp.int32, (8, 128), 1)
    total = r_ref.shape[3]
    for k in range(n_gy):
        for p in range(2):
            tile = None
            for c in range(3):
                shift = (span * c - (nz * k - 4)) % total
                piece = (pltpu.roll(mine[c, p], shift, axis=1) if shift else mine[c, p])[:, :128]
                tile = piece if tile is None else jnp.where(lane >= span * c, piece, tile)
            win[k, p] = tile
    windows = []
    for j in [k for k in sorted(range(n_gy), key=lambda j: (abs(j % 4 - 2), -min(j, n_gy - j))) if k]:
        peer = at(0, j)
        windows.append(message(win.at[peer[1]], in_win.at[gy], peer))
    in_win[gy] = win[gy]

    for ref, parts in (
            (res_right, [mine[1, 0], mine[2, 0], mine[0, 1], mine[1, 1], mine[2, 1]]),
            (res_left, [mine[0, 0], mine[1, 0], mine[2, 0]]),
            (res_upper, pack_rows([(mine[key], 7) for key in cells] + [(mine[c, p], 6) for c in (0, 2) for p in range(2)])),
            (res_lower, pack_rows([(mine[key], 0) for key in cells])),
            (rr_upper, pack_rows([(mine[c, 1], 7) for c in range(3)])),
            (rr_lower, pack_rows([(mine[c, 1], 0) for c in range(3)] + [(mine[1, 0], 0)])),
            (rl_upper, pack_rows([(mine[c, 0], 7) for c in range(3)] + [(mine[0, 0], 6)])),
            (rl_lower, pack_rows([(mine[c, 0], 0) for c in range(2)]))):
        for i, part in enumerate(parts):
            ref[i] = part
    second = [
        message(rr_upper, in_rl_below, at(1, 1)), message(rr_lower, in_rl_above, at(1, -1)),
        message(rl_upper, in_rr_below, at(-1, 1)), message(rl_lower, in_rr_above, at(-1, -1)),
        message(res_right, in_res_left, at(1, 0)), message(res_left, in_res_right, at(-1, 0)),
        message(res_upper, in_res_below, at(0, 1)), message(res_lower, in_res_above, at(0, -1)),
    ]


    for copy in windows + edge_halo:
        copy.wait_recv()
    passed_on = [message(in_win.at[:, 1], in_win_left, at(1, 0)), message(in_win.at[:, 0], in_win_right, at(-1, 0))]
    both = {}
    for i, (c, p) in enumerate(cells):
        places = [(in_e_next, i, 0)] + [(in_e_prev, p, 7)] * (c == 2)
        both[c, p] = joined(wrapped(em_ref[c, p]) * wrapped(es_ref[c, p]), with_rows(None, *places))
    node = {p: joined(wrapped(ns_ref[p]), with_rows(None, (in_e_next, 6 + p, 0))) for p in range(2)}
    both[0, -1] = joined(in_e_left[0], in_e_cb[0])
    for c in range(3):
        both[c, 2] = joined(in_e_right[c], in_e_ca[0])
    node[2] = joined(in_e_right[3], in_e_ca[0])
    for copy in second + scale_halo:
        copy.wait_recv()

    def ef_halo(ref, count, i):
        tile = ref[count]
        return joined(ref[i], pltpu.roll(tile, 8 - 2 * i, axis=0) if i else tile)

    for i, (c, p) in enumerate(cells):
        rows = [(in_res_below, i, 7), (in_res_above, i, 0)] + [(in_res_below, 6 + c + p, 6)] * (c != 1)
        res[c, p] = joined(mine[c, p], with_rows(None, *rows))
    res[1, -2] = joined(in_res_left[0], with_rows(None, (in_rl_above, 3, 0)))
    res[2, -2] = joined(in_res_left[1], in_res_left[1])
    for c in range(3):
        res[c, -1] = joined(in_res_left[2 + c], with_rows(None, (in_rl_below, c, 7), (in_rl_above, c, 0)))
        rows = [(in_rr_below, c, 7)] + [(in_rr_below, 3, 6)] * (c == 0) + [(in_rr_above, c, 0)] * (c < 2)
        res[c, 2] = joined(in_res_right[c], with_rows(None, *rows))
    scale = {(c, p): faced[p, c] for c in range(3) for p in range(2)}
    for c in range(3):
        scale[c, -1] = ef_halo(in_ef_left, 3, c)
    for c in range(1, 3):
        scale[c, 2] = ef_halo(in_ef_right, 2, c - 1)
    sm = {key: scale[key] * curl_adjoint(res, *key, FACE) for key in scale}
    new = {key: tt[key] + curl(sm, *key, FACE) for key in tt}
    div3 = {p: divergence(new, p) for p in range(-1, 2)}
    for c in range(3):
        for p in range(2):
            key = (c, p)
            out = new[key] + damping * (rr[key] - apply_faces(new, div3, c, p)) / dd[key]
            vel_ref[c, p] = out[0:8]

    store = [pltpu.make_async_copy(vel_ref, vel_hbm, load_sem.at[5]), pltpu.make_async_copy(ec_ref, ec_hbm, load_sem.at[6])]
    store[0].start()
    for copy in passed_on:
        copy.wait_recv()
    g = {}
    for p, ref in ((-1, in_win_left), (0, None), (1, None), (2, in_win_right)):
        rows = (in_win[:, p] if ref is None else ref[...]).reshape(ny, 128)
        turned = jnp.concatenate([rows, rows[:16], rows[ny - 16:]], axis=0).T
        for c in range(3):
            g[c, p] = pltpu.roll(turned[span * c:span * c + span], span - 4, axis=0)
    edge_residual = {key: curl_adjoint(g, *key, EDGE) for key in both}
    ww = {key: both[key] * edge_residual[key] for key in both}
    pot = {}
    for p in range(3):
        adjoint = ((ww[0, p - 1] - ww[0, p]) + (down(ww[1, p], 1) - ww[1, p])) + (down(ww[2, p], 0) - ww[2, p])
        pot[0, p] = node[p] * -adjoint
    for c in range(3):
        for p in range(2):
            ahead = pot[0, p + 1] if c == 0 else up(pot[0, p], EDGE[c - 1])
            smoothed = wrapped(es_ref[c, p]) * edge_residual[c, p][:nz]
            ec_ref[c, p] = (smoothed + (ahead - pot[0, p])[:nz])[:, :ny]
    store[1].start()
    for copy in sent:
        copy.wait_send()
    for copy in store:
        copy.wait()


def hand_over(a, b, a_out, b_out):
    a_out[...] = a[...]
    b_out[...] = b[...]


def on_device(right_side, face_mass, edge_scale, edge_mass, node_scale):
    n_gx, n_gy = lax.axis_size("gx"), lax.axis_size("gy")
    edge_scale, edge_mass, node_scale = (jnp.swapaxes(a, -1, -2) for a in (edge_scale, edge_mass, node_scale))
    total, nz = right_side.shape[3], edge_scale.shape[2]

    def own(a):
        return pltpu.VMEM(a.shape, jnp.float32)

    def rows(*lead):
        return pltpu.VMEM((*lead, 8, total), jnp.float32)

    def tile(*lead):
        return pltpu.VMEM((*lead, 8, 128), jnp.float32)

    def field(*lead):
        return pltpu.VMEM((*lead, nz, 128), jnp.float32)

    arguments = (right_side, face_mass, edge_scale, edge_mass, node_scale)
    first = [rows(7), rows(4), rows(3), rows(2), rows(1), rows(1), rows(1), rows(1)]
    second = [rows(5), rows(3), rows(2), rows(1), rows(1), rows(1), rows(1), rows(1)]
    halo = [field(4), field(1), tile(1), tile(1), tile(1), tile(1)]
    count = 24 + 5 * n_gy - 2
    velocity, correction = pl.pallas_call(
        functools.partial(kernel, n_gx, n_gy),
        out_shape=(jax.ShapeDtypeStruct(right_side.shape, jnp.float32),
                   jax.ShapeDtypeStruct(edge_scale.shape, jnp.float32)),
        in_specs=[pl.BlockSpec(memory_space=pltpu.HBM)] * 5,
        out_specs=(pl.BlockSpec(memory_space=pl.ANY),) * 2,
        scratch_shapes=[own(a) for a in (*arguments, right_side, edge_scale)] + first + first + [
            tile(n_gy, 2), tile(n_gy, 2), pltpu.VMEM((2, 3, 16, total), jnp.float32),
            rows(4), rows(3), rows(4), rows(3)] + halo + halo + [
            *second, *second, tile(n_gy, 2), tile(n_gy, 2), tile(n_gy), tile(n_gy),
            pltpu.SemaphoreType.DMA((7,)),
            pltpu.SemaphoreType.DMA((count,)), pltpu.SemaphoreType.DMA((count,)),
        ],
        compiler_params=pltpu.CompilerParams(
            collective_id=0, has_side_effects=True, vmem_limit_bytes=60 * 1024 * 1024),
    )(*arguments)
    inside = pl.BlockSpec(memory_space=pltpu.VMEM)
    velocity, correction = pl.pallas_call(
        hand_over,
        out_shape=(jax.ShapeDtypeStruct(velocity.shape, jnp.float32),
                   jax.ShapeDtypeStruct(correction.shape, jnp.float32)),
        in_specs=[inside, inside],
        out_specs=(inside, inside),
        compiler_params=pltpu.CompilerParams(vmem_limit_bytes=60 * 1024 * 1024),
    )(velocity, correction)
    return velocity, jnp.swapaxes(correction, 2, 3)


def solution(mesh):
    placed = (
        P(None, "gx", "gy", None),
        P(None, "gx", "gy", None),
        P(None, "gx", None, "gy"),
        P(None, "gx", None, "gy"),
        P("gx", None, "gy"),
    )
    return jax.shard_map(
        on_device,
        mesh=mesh,
        in_specs=placed,
        out_specs=(P(None, "gx", "gy", None), P(None, "gx", None, "gy")),
        check_vma=False,
    )
```

```python
import functools

import jax
import jax.numpy as jnp
from jax import lax
from jax.experimental import pallas as pl
from jax.experimental.pallas import tpu as pltpu
from jax.sharding import PartitionSpec as P

MESH = pl.DeviceIdType.MESH
grad_div_weight = 1.0
damping = 0.3


def up(a, axis):
    return pltpu.roll(a, a.shape[axis] - 1, axis=axis)


def down(a, axis):
    return pltpu.roll(a, 1, axis=axis)


def half_turn(a):
    return pltpu.roll(a, 4, axis=0)


def sublane(shape):
    return lax.broadcasted_iota(jnp.int32, shape, len(shape) - 2)


def shift_up(u, c, p, direction, axes):
    return u[c, p + 1] if direction == 0 else up(u[c, p], axes[direction - 1])


def shift_down(u, c, p, direction, axes):
    return u[c, p - 1] if direction == 0 else down(u[c, p], axes[direction - 1])


FACE = (0, 1)
EDGE = (1, 0)


def curl(u, c, p, axes):
    a, b = (c + 1) % 3, (c + 2) % 3
    return (shift_up(u, b, p, a, axes) - u[b, p]) - (shift_up(u, a, p, b, axes) - u[a, p])


def curl_adjoint(g, a, p, axes):
    b, c = (a + 1) % 3, (a + 2) % 3
    return (shift_down(g, b, p, c, axes) - g[b, p]) - (shift_down(g, c, p, b, axes) - g[c, p])


def turn(a, by):
    return pltpu.roll(a, by % 8, axis=0) if by % 8 else a


def pack_rows(items):
    packed = []
    for base in range(0, len(items), 8):
        tile = None
        for slot, (a, row) in enumerate(items[base:base + 8]):
            piece = turn(a, slot - row)
            tile = piece if tile is None else jnp.where(sublane(a.shape) == slot, piece, tile)
        packed.append(tile)
    return packed


def with_rows(tile, *items):
    for ref, slot, row in items:
        piece = turn(ref[slot // 8], row - slot % 8)
        tile = piece if tile is None else jnp.where(sublane(piece.shape) == row, piece, tile)
    return tile


def joined(own_part, halo):
    return jnp.concatenate([own_part, halo], axis=0)


def kernel(n_gx, n_gy, r_hbm, fm_hbm, es_hbm, em_hbm, ns_hbm, vel_hbm, ec_hbm,
           r_ref, fm_ref, es_ref, em_ref, ns_ref, vel_ref, ec_ref,
           x_right, x_left, y_upper, y_lower, cr_upper, cr_lower, cl_upper, cl_lower,
           in_left, in_right, in_below, in_above, in_cl_below, in_cl_above, in_cr_below, in_cr_above,
           es_out, es_in, faced, ef_right, ef_left, in_ef_left, in_ef_right,
           e_left, e_right, e_next, e_prev, e_ca, e_cb, in_e_right, in_e_left, in_e_next, in_e_prev, in_e_ca, in_e_cb,
           res_right, res_left, res_upper, res_lower, rr_upper, rr_lower, rl_upper, rl_lower,
           in_res_left, in_res_right, in_res_below, in_res_above, in_rl_below, in_rl_above, in_rr_below, in_rr_above, win, in_win, in_win_right, in_win_left,
           load_sem, send_sem, recv_sem):
    gx, gy = lax.axis_index("gx"), lax.axis_index("gy")

    def at(dx, dy):
        return (lax.rem(gx + dx + n_gx, n_gx), lax.rem(gy + dy + n_gy, n_gy))

    barrier = pltpu.get_barrier_semaphore()
    greeted = [at(a, b) for a in (1, -1) for b in (-1, 0, 1)] + [at(0, j) for j in range(1, n_gy)]
    for peer in greeted:
        pl.semaphore_signal(barrier, inc=1, device_id=peer, device_id_type=MESH)
    loads = [pltpu.make_async_copy(src, dst, load_sem.at[i]) for i, (src, dst) in enumerate(
        ((r_hbm, r_ref), (fm_hbm, fm_ref), (es_hbm, es_ref), (em_hbm, em_ref), (ns_hbm, ns_ref)))]
    for load in loads:
        load.start()
    sent = []

    def message(src, dst, peer):
        index = len(sent)
        copy = pltpu.make_async_remote_copy(
            src_ref=src, dst_ref=dst, send_sem=send_sem.at[index], recv_sem=recv_sem.at[index],
            device_id=peer, device_id_type=MESH)
        sent.append(copy)
        copy.start()
        return copy

    for load in loads[:2]:
        load.wait()
    r = [[r_ref[c, p] for p in range(2)] for c in range(3)]
    fm = [[fm_ref[c, p] for p in range(2)] for c in range(3)]
    s1 = [[damping * r[c][p] / (fm[c][p] + 2.0 * grad_div_weight) for p in range(2)] for c in range(3)]
    known = [s1[0][1] - s1[0][0], up(s1[2][0], 1) - s1[2][0]]
    wide = sublane(known[0].shape)
    partial = known[0] + (jnp.where(wide == 7, 0.0, up(s1[1][0], 0)) - s1[1][0]) + known[1]
    to_right = [r[c][1] for c in range(3)] + [fm[c][1] for c in range(3)] + [partial]
    to_left = [r[0][0], fm[0][0], known[0] + known[1], s1[1][0]]
    cells = [(c, p) for c in range(3) for p in range(2)]
    for ref, parts in (
            (x_right, to_right), (x_left, to_left),
            (y_upper, pack_rows([(f[c][p], 7) for f in (r, fm) for c, p in cells] + [(s1[c][p], 6) for c, p in cells])),
            (y_lower, pack_rows([(f[p], 0) for f in (r[1], fm[1], s1[0], s1[2]) for p in range(2)]
                                + [(s1[1][p], 1) for p in range(2)])),
            (cr_upper, pack_rows([(s1[c][1], 7) for c in range(3)])),
            (cr_lower, pack_rows([(r[1][1], 0), (fm[1][1], 0), (s1[0][1], 0), (s1[2][1], 0), (s1[1][1], 1), (s1[1][0], 0)])),
            (cl_upper, pack_rows([(to_left[i], 7) for i in range(4)] + [(s1[0][0], 6)])),
            (cl_lower, pack_rows([(s1[1][0], 0), (s1[0][0], 0)]))):
        for i, part in enumerate(parts):
            ref[i] = part

    for load in loads[2:]:
        load.wait()
    nz, ny = es_ref.shape[2], es_ref.shape[3]

    def wrapped(field):
        return jnp.concatenate([field, field[:, :16], field[:, ny - 16:]], axis=1)

    es = {(c, p): wrapped(es_ref[c, p]) for c in range(3) for p in range(2)}
    em = {(c, p): wrapped(em_ref[c, p]) for c in range(3) for p in range(2)}
    ns = {p: wrapped(ns_ref[p]) for p in range(2)}
    products = {key: em[key] * es[key] for key in es}
    for i, field in enumerate([products[c, 0] for c in range(3)] + [ns[0]]):
        e_left[i] = field
    e_right[0] = products[0, 1]
    e_next[0] = pack_rows([(field[0:8], 0) for field in [products[key] for key in cells] + [ns[0], ns[1]]])[0]
    e_prev[0] = pack_rows([(products[2, p][nz - 8:], 7) for p in range(2)])[0]
    e_ca[0] = products[2, 0][nz - 8:]
    e_cb[0] = products[0, 1][0:8]

    order = [(c, p) for p in range(2) for c in range(3)]
    sub = sublane((8, 128))
    halos = []
    for t in range(2):
        group = [es[key] for key in order[4 * t:4 * t + 4]]
        group += [group[0]] * (4 - len(group))
        turned = jnp.concatenate(group, axis=0).T
        es_out[:, t] = turned[:ny].reshape(n_gy, 8, 128)
        after = turned[8:ny + 8].reshape(n_gy, 8, 128)
        before = jnp.concatenate([turned[ny - 8:ny], turned[:ny - 8]], axis=0).reshape(n_gy, 8, 128)
        halos.append((after, before))
    column = lax.broadcasted_iota(jnp.int32, (8, 128), 1)
    for k in range(n_gy):
        upper = jnp.where(sub < 4, halos[0][0][k], halos[0][1][k])
        lower = jnp.where(sub < 4, halos[1][0][k], halos[1][1][k])
        spare = jnp.where((sub == 1) | (sub == 2), turn(upper, 2), pltpu.roll(upper, 2 * nz, axis=1))
        spare = jnp.where((sub == 3) | (sub == 4), half_turn(pltpu.roll(lower, 2 * nz, axis=1)), spare)
        es_out[k, 1] = jnp.where(column < 2 * nz, es_out[k, 1], spare)

    pl.semaphore_wait(barrier, len(greeted))

    first = [
        message(cr_upper, in_cl_below, at(1, 1)), message(cr_lower, in_cl_above, at(1, -1)),
        message(cl_upper, in_cr_below, at(-1, 1)), message(cl_lower, in_cr_above, at(-1, -1)),
        message(x_left, in_right, at(-1, 0)), message(x_right, in_left, at(1, 0)),
        message(y_upper, in_below, at(0, 1)), message(y_lower, in_above, at(0, -1)),
    ]
    exchange = []
    for j in [k for k in sorted(range(n_gy), key=lambda j: (abs(j % 4 - 2), -min(j, n_gy - j))) if k]:
        peer = at(0, j)
        exchange.append(message(es_out.at[peer[1]], es_in.at[gy], peer))
    es_in[gy] = es_out[gy]
    edge_halo = [
        message(e_left, in_e_right, at(-1, 0)), message(e_right, in_e_left, at(1, 0)),
        message(e_next, in_e_next, at(0, -1)), message(e_prev, in_e_prev, at(0, 1)),
        message(e_ca, in_e_ca, at(-1, 1)), message(e_cb, in_e_cb, at(1, -1)),
    ]

    for copy in exchange:
        copy.wait_recv()
    lane4 = lax.broadcasted_iota(jnp.int32, (8, 128), 1) // nz
    total = r_ref.shape[3]
    for i, (c, p) in enumerate(order):
        t, q = divmod(i, 4)
        for m in range(total // 128):
            for h in range(2):
                tile = None
                for jj in range(4):
                    piece = es_in[4 * m + jj, 1 if h else t]
                    place = 2 + i % 2 if h else q
                    if jj != place:
                        piece = pltpu.roll(piece, (nz * (jj - place)) % 128, axis=1)
                    tile = piece if tile is None else jnp.where(lane4 == jj, piece, tile)
                faced[p, c, 8 * h:8 * h + 8, 128 * m:128 * m + 128] = turn(tile, -2 * (i // 2)) if h else tile
    for ref, p, comps in ((ef_right, 1, (0, 1, 2)), (ef_left, 0, (1, 2))):
        tile = None
        for i, c in enumerate(comps):
            ref[i] = faced[p, c, 0:8]
            piece = faced[p, c, 8:16]
            piece = pltpu.roll(piece, 2 * i, axis=0) if i else piece
            tile = piece if tile is None else jnp.where((wide == 2 * i) | (wide == 2 * i - 1), piece, tile)
        ref[len(comps)] = tile
    scale_halo = [message(ef_right, in_ef_left, at(1, 0)), message(ef_left, in_ef_right, at(-1, 0))]

    for copy in first:
        copy.wait_recv()

    rr, ff, dd, ss = {}, {}, {}, {}
    for i, (c, p) in enumerate(cells):
        above = c == 1
        rr[c, p] = joined(r_ref[c, p], with_rows(None, (in_below, i, 7), *[(in_above, p, 0)] * above))
        ff[c, p] = joined(fm_ref[c, p], with_rows(None, (in_below, 6 + i, 7), *[(in_above, 2 + p, 0)] * above))
    for c in range(3):
        rr[c, -1] = joined(in_left[c], with_rows(None, (in_cl_above, 0, 0)) if c == 1 else in_left[c])
        ff[c, -1] = joined(in_left[3 + c], with_rows(None, (in_cl_above, 1, 0)) if c == 1 else in_left[3 + c])
    rr[0, 2] = joined(in_right[0], with_rows(None, (in_cr_below, 0, 7)))
    ff[0, 2] = joined(in_right[1], with_rows(None, (in_cr_below, 1, 7)))
    for key in rr:
        dd[key] = ff[key] + 2.0 * grad_div_weight
        ss[key] = damping * rr[key] / dd[key]

    def more_rows(key, *items):
        ss[key] = joined(ss[key][0:8], with_rows(ss[key][8:16], *items))

    for i, (c, p) in enumerate(cells):
        more_rows((c, p), (in_below, 12 + i, 6), (in_above, (4, 8, 6)[c] + p, 1 if c == 1 else 0))
    for c in range(3):
        more_rows((c, -1), (in_cl_below, c, 7), (in_cl_above, (2, 4, 3)[c], 1 if c == 1 else 0))
    more_rows((0, 2), (in_cr_below, 4, 6), (in_cr_above, 1, 0))
    known = joined(in_right[2], with_rows(None, (in_cr_below, 2, 7)))
    second_flux = joined(in_right[3], with_rows(None, (in_cr_below, 3, 7), (in_cr_above, 0, 0)))

    def divergence(u, p):
        return (u[0, p + 1] - u[0, p]) + (up(u[1, p], 0) - u[1, p]) + (up(u[2, p], 1) - u[2, p])

    def apply_faces(u, div, c, p):
        shifted = div[p - 1] if c == 0 else down(div[p], c - 1)
        return ff[c, p] * u[c, p] + grad_div_weight * (shifted - div[p])

    div1 = {p: divergence(ss, p) for p in range(-1, 2)}
    div1[2] = known + (up(second_flux, 0) - second_flux)
    far = in_left[6]
    far = jnp.where(wide == 7, far + turn(in_cl_above[0], 2), far)
    div1[-2] = joined(far, far)
    tt = {key: ss[key] + damping * (rr[key] - apply_faces(ss, div1, *key)) / dd[key] for key in rr}
    div2 = {p: divergence(tt, p) for p in range(-1, 2)}
    res = {(c, p): rr[c, p] - apply_faces(tt, div2, c, p) for c in range(3) for p in range(2)}

    mine = {key: res[key][0:8] for key in res}
    span = nz + 8
    lane = lax.broadcasted_iota(jnp.int32, (8, 128), 1)
    total = r_ref.shape[3]
    for k in range(n_gy):
        for p in range(2):
            tile = None
            for c in range(3):
                shift = (span * c - (nz * k - 4)) % total
                piece = (pltpu.roll(mine[c, p], shift, axis=1) if shift else mine[c, p])[:, :128]
                tile = piece if tile is None else jnp.where(lane >= span * c, piece, tile)
            win[k, p] = tile
    windows = []
    for j in [k for k in sorted(range(n_gy), key=lambda j: (abs(j % 4 - 2), -min(j, n_gy - j))) if k]:
        peer = at(0, j)
        windows.append(message(win.at[peer[1]], in_win.at[gy], peer))
    in_win[gy] = win[gy]

    for ref, parts in (
            (res_right, [mine[1, 0], mine[2, 0], mine[0, 1], mine[1, 1], mine[2, 1]]),
            (res_left, [mine[0, 0], mine[1, 0], mine[2, 0]]),
            (res_upper, pack_rows([(mine[key], 7) for key in cells] + [(mine[c, p], 6) for c in (0, 2) for p in range(2)])),
            (res_lower, pack_rows([(mine[key], 0) for key in cells])),
            (rr_upper, pack_rows([(mine[c, 1], 7) for c in range(3)])),
            (rr_lower, pack_rows([(mine[c, 1], 0) for c in range(3)] + [(mine[1, 0], 0)])),
            (rl_upper, pack_rows([(mine[c, 0], 7) for c in range(3)] + [(mine[0, 0], 6)])),
            (rl_lower, pack_rows([(mine[c, 0], 0) for c in range(2)]))):
        for i, part in enumerate(parts):
            ref[i] = part
    second = [
        message(rr_upper, in_rl_below, at(1, 1)), message(rr_lower, in_rl_above, at(1, -1)),
        message(rl_upper, in_rr_below, at(-1, 1)), message(rl_lower, in_rr_above, at(-1, -1)),
        message(res_right, in_res_left, at(1, 0)), message(res_left, in_res_right, at(-1, 0)),
        message(res_upper, in_res_below, at(0, 1)), message(res_lower, in_res_above, at(0, -1)),
    ]


    for copy in windows:
        copy.wait_recv()
    passed_on = [message(in_win.at[:, 1], in_win_left, at(1, 0)), message(in_win.at[:, 0], in_win_right, at(-1, 0))]
    for copy in edge_halo:
        copy.wait_recv()
    both = {}
    for i, (c, p) in enumerate(cells):
        places = [(in_e_next, i, 0)] + [(in_e_prev, p, 7)] * (c == 2)
        both[c, p] = joined(wrapped(em_ref[c, p]) * wrapped(es_ref[c, p]), with_rows(None, *places))
    node = {p: joined(wrapped(ns_ref[p]), with_rows(None, (in_e_next, 6 + p, 0))) for p in range(2)}
    both[0, -1] = joined(in_e_left[0], in_e_cb[0])
    for c in range(3):
        both[c, 2] = joined(in_e_right[c], in_e_ca[0])
    node[2] = joined(in_e_right[3], in_e_ca[0])
    for copy in second + scale_halo:
        copy.wait_recv()

    def ef_halo(ref, count, i):
        tile = ref[count]
        return joined(ref[i], pltpu.roll(tile, 8 - 2 * i, axis=0) if i else tile)

    for i, (c, p) in enumerate(cells):
        rows = [(in_res_below, i, 7), (in_res_above, i, 0)] + [(in_res_below, 6 + c + p, 6)] * (c != 1)
        res[c, p] = joined(mine[c, p], with_rows(None, *rows))
    res[1, -2] = joined(in_res_left[0], with_rows(None, (in_rl_above, 3, 0)))
    res[2, -2] = joined(in_res_left[1], in_res_left[1])
    for c in range(3):
        res[c, -1] = joined(in_res_left[2 + c], with_rows(None, (in_rl_below, c, 7), (in_rl_above, c, 0)))
        rows = [(in_rr_below, c, 7)] + [(in_rr_below, 3, 6)] * (c == 0) + [(in_rr_above, c, 0)] * (c < 2)
        res[c, 2] = joined(in_res_right[c], with_rows(None, *rows))
    scale = {(c, p): faced[p, c] for c in range(3) for p in range(2)}
    for c in range(3):
        scale[c, -1] = ef_halo(in_ef_left, 3, c)
    for c in range(1, 3):
        scale[c, 2] = ef_halo(in_ef_right, 2, c - 1)
    sm = {key: scale[key] * curl_adjoint(res, *key, FACE) for key in scale}
    new = {key: tt[key] + curl(sm, *key, FACE) for key in tt}
    div3 = {p: divergence(new, p) for p in range(-1, 2)}
    for c in range(3):
        for p in range(2):
            key = (c, p)
            out = new[key] + damping * (rr[key] - apply_faces(new, div3, c, p)) / dd[key]
            vel_ref[c, p] = out[0:8]

    store = [pltpu.make_async_copy(vel_ref, vel_hbm, load_sem.at[5]), pltpu.make_async_copy(ec_ref, ec_hbm, load_sem.at[6])]
    store[0].start()
    for copy in passed_on:
        copy.wait_recv()
    g = {}
    for p, ref in ((-1, in_win_left), (0, None), (1, None), (2, in_win_right)):
        rows = (in_win[:, p] if ref is None else ref[...]).reshape(ny, 128)
        turned = jnp.concatenate([rows, rows[:16], rows[ny - 16:]], axis=0).T
        for c in range(3):
            g[c, p] = pltpu.roll(turned[span * c:span * c + span], span - 4, axis=0)
    edge_residual = {key: curl_adjoint(g, *key, EDGE) for key in both}
    ww = {key: both[key] * edge_residual[key] for key in both}
    pot = {}
    for p in range(3):
        adjoint = ((ww[0, p - 1] - ww[0, p]) + (down(ww[1, p], 1) - ww[1, p])) + (down(ww[2, p], 0) - ww[2, p])
        pot[0, p] = node[p] * -adjoint
    for c in range(3):
        for p in range(2):
            ahead = pot[0, p + 1] if c == 0 else up(pot[0, p], EDGE[c - 1])
            smoothed = wrapped(es_ref[c, p]) * edge_residual[c, p][:nz]
            ec_ref[c, p] = (smoothed + (ahead - pot[0, p])[:nz])[:, :ny]
    store[1].start()
    for copy in sent:
        copy.wait_send()
    for copy in store:
        copy.wait()


def hand_over(a, b, a_out, b_out):
    a_out[...] = a[...]
    b_out[...] = b[...]


def on_device(right_side, face_mass, edge_scale, edge_mass, node_scale):
    n_gx, n_gy = lax.axis_size("gx"), lax.axis_size("gy")
    edge_scale, edge_mass, node_scale = (jnp.swapaxes(a, -1, -2) for a in (edge_scale, edge_mass, node_scale))
    total, nz = right_side.shape[3], edge_scale.shape[2]

    def own(a):
        return pltpu.VMEM(a.shape, jnp.float32)

    def rows(*lead):
        return pltpu.VMEM((*lead, 8, total), jnp.float32)

    def tile(*lead):
        return pltpu.VMEM((*lead, 8, 128), jnp.float32)

    def field(*lead):
        return pltpu.VMEM((*lead, nz, 128), jnp.float32)

    arguments = (right_side, face_mass, edge_scale, edge_mass, node_scale)
    first = [rows(7), rows(4), rows(3), rows(2), rows(1), rows(1), rows(1), rows(1)]
    second = [rows(5), rows(3), rows(2), rows(1), rows(1), rows(1), rows(1), rows(1)]
    halo = [field(4), field(1), tile(1), tile(1), tile(1), tile(1)]
    count = 24 + 5 * n_gy - 2
    velocity, correction = pl.pallas_call(
        functools.partial(kernel, n_gx, n_gy),
        out_shape=(jax.ShapeDtypeStruct(right_side.shape, jnp.float32),
                   jax.ShapeDtypeStruct(edge_scale.shape, jnp.float32)),
        in_specs=[pl.BlockSpec(memory_space=pltpu.HBM)] * 5,
        out_specs=(pl.BlockSpec(memory_space=pl.ANY),) * 2,
        scratch_shapes=[own(a) for a in (*arguments, right_side, edge_scale)] + first + first + [
            tile(n_gy, 2), tile(n_gy, 2), pltpu.VMEM((2, 3, 16, total), jnp.float32),
            rows(4), rows(3), rows(4), rows(3)] + halo + halo + [
            *second, *second, tile(n_gy, 2), tile(n_gy, 2), tile(n_gy), tile(n_gy),
            pltpu.SemaphoreType.DMA((7,)),
            pltpu.SemaphoreType.DMA((count,)), pltpu.SemaphoreType.DMA((count,)),
        ],
        compiler_params=pltpu.CompilerParams(
            collective_id=0, has_side_effects=True, vmem_limit_bytes=60 * 1024 * 1024),
    )(*arguments)
    inside = pl.BlockSpec(memory_space=pltpu.VMEM)
    velocity, correction = pl.pallas_call(
        hand_over,
        out_shape=(jax.ShapeDtypeStruct(velocity.shape, jnp.float32),
                   jax.ShapeDtypeStruct(correction.shape, jnp.float32)),
        in_specs=[inside, inside],
        out_specs=(inside, inside),
        compiler_params=pltpu.CompilerParams(vmem_limit_bytes=60 * 1024 * 1024),
    )(velocity, correction)
    return velocity, jnp.swapaxes(correction, 2, 3)


def solution(mesh):
    placed = (
        P(None, "gx", "gy", None),
        P(None, "gx", "gy", None),
        P(None, "gx", None, "gy"),
        P(None, "gx", None, "gy"),
        P("gx", None, "gy"),
    )
    return jax.shard_map(
        on_device,
        mesh=mesh,
        in_specs=placed,
        out_specs=(P(None, "gx", "gy", None), P(None, "gx", None, "gy")),
        check_vma=False,
    )
```

```python
import functools

import jax
import jax.numpy as jnp
from jax import lax
from jax.experimental import pallas as pl
from jax.experimental.pallas import tpu as pltpu
from jax.sharding import PartitionSpec as P

MESH = pl.DeviceIdType.MESH
grad_div_weight = 1.0
damping = 0.3


def up(a, axis):
    return pltpu.roll(a, a.shape[axis] - 1, axis=axis)


def down(a, axis):
    return pltpu.roll(a, 1, axis=axis)


def half_turn(a):
    return pltpu.roll(a, 4, axis=0)


def sublane(shape):
    return lax.broadcasted_iota(jnp.int32, shape, len(shape) - 2)


def shift_up(u, c, p, direction, axes):
    return u[c, p + 1] if direction == 0 else up(u[c, p], axes[direction - 1])


def shift_down(u, c, p, direction, axes):
    return u[c, p - 1] if direction == 0 else down(u[c, p], axes[direction - 1])


FACE = (0, 1)
EDGE = (1, 0)


def curl(u, c, p, axes):
    a, b = (c + 1) % 3, (c + 2) % 3
    return (shift_up(u, b, p, a, axes) - u[b, p]) - (shift_up(u, a, p, b, axes) - u[a, p])


def curl_adjoint(g, a, p, axes):
    b, c = (a + 1) % 3, (a + 2) % 3
    return (shift_down(g, b, p, c, axes) - g[b, p]) - (shift_down(g, c, p, b, axes) - g[c, p])


def turn(a, by):
    return pltpu.roll(a, by % 8, axis=0) if by % 8 else a


def pack_rows(items):
    packed = []
    for base in range(0, len(items), 8):
        tile = None
        for slot, (a, row) in enumerate(items[base:base + 8]):
            piece = turn(a, slot - row)
            tile = piece if tile is None else jnp.where(sublane(a.shape) == slot, piece, tile)
        packed.append(tile)
    return packed


def with_rows(tile, *items):
    for ref, slot, row in items:
        piece = turn(ref[slot // 8], row - slot % 8)
        tile = piece if tile is None else jnp.where(sublane(piece.shape) == row, piece, tile)
    return tile


def joined(own_part, halo):
    return jnp.concatenate([own_part, halo], axis=0)


def kernel(n_gx, n_gy, r_hbm, fm_hbm, es_hbm, em_hbm, ns_hbm, vel_hbm, ec_hbm,
           r_ref, fm_ref, es_ref, em_ref, ns_ref, vel_ref, ec_ref,
           x_right, x_left, y_upper, y_lower, cr_upper, cr_lower, cl_upper, cl_lower,
           in_left, in_right, in_below, in_above, in_cl_below, in_cl_above, in_cr_below, in_cr_above,
           es_out, es_in, faced, ef_right, ef_left, in_ef_left, in_ef_right,
           e_left, e_right, e_next, e_prev, e_ca, e_cb, in_e_right, in_e_left, in_e_next, in_e_prev, in_e_ca, in_e_cb,
           res_right, res_left, res_upper, res_lower, rr_upper, rr_lower, rl_upper, rl_lower,
           in_res_left, in_res_right, in_res_below, in_res_above, in_rl_below, in_rl_above, in_rr_below, in_rr_above, win, in_win, in_win_right, in_win_left,
           load_sem, send_sem, recv_sem):
    gx, gy = lax.axis_index("gx"), lax.axis_index("gy")

    def at(dx, dy):
        return (lax.rem(gx + dx + n_gx, n_gx), lax.rem(gy + dy + n_gy, n_gy))

    barrier = pltpu.get_barrier_semaphore()
    greeted = [at(a, b) for a in (1, -1) for b in (-1, 0, 1)] + [at(0, j) for j in range(1, n_gy)]
    for peer in greeted:
        pl.semaphore_signal(barrier, inc=1, device_id=peer, device_id_type=MESH)
    loads = [pltpu.make_async_copy(src, dst, load_sem.at[i]) for i, (src, dst) in enumerate(
        ((r_hbm, r_ref), (fm_hbm, fm_ref), (es_hbm, es_ref), (em_hbm, em_ref), (ns_hbm, ns_ref)))]
    for load in loads:
        load.start()
    sent = []

    def message(src, dst, peer):
        index = len(sent)
        copy = pltpu.make_async_remote_copy(
            src_ref=src, dst_ref=dst, send_sem=send_sem.at[index], recv_sem=recv_sem.at[index],
            device_id=peer, device_id_type=MESH)
        sent.append(copy)
        copy.start()
        return copy

    for load in loads[:2]:
        load.wait()
    r = [[r_ref[c, p] for p in range(2)] for c in range(3)]
    fm = [[fm_ref[c, p] for p in range(2)] for c in range(3)]
    s1 = [[damping * r[c][p] / (fm[c][p] + 2.0 * grad_div_weight) for p in range(2)] for c in range(3)]
    known = [s1[0][1] - s1[0][0], up(s1[2][0], 1) - s1[2][0]]
    wide = sublane(known[0].shape)
    partial = known[0] + (jnp.where(wide == 7, 0.0, up(s1[1][0], 0)) - s1[1][0]) + known[1]
    to_right = [r[c][1] for c in range(3)] + [fm[c][1] for c in range(3)] + [partial]
    to_left = [r[0][0], fm[0][0], known[0] + known[1], s1[1][0]]
    cells = [(c, p) for c in range(3) for p in range(2)]
    for ref, parts in (
            (x_right, to_right), (x_left, to_left),
            (y_upper, pack_rows([(f[c][p], 7) for f in (r, fm) for c, p in cells] + [(s1[c][p], 6) for c, p in cells])),
            (y_lower, pack_rows([(f[p], 0) for f in (r[1], fm[1], s1[0], s1[2]) for p in range(2)]
                                + [(s1[1][p], 1) for p in range(2)])),
            (cr_upper, pack_rows([(s1[c][1], 7) for c in range(3)])),
            (cr_lower, pack_rows([(r[1][1], 0), (fm[1][1], 0), (s1[0][1], 0), (s1[2][1], 0), (s1[1][1], 1), (s1[1][0], 0)])),
            (cl_upper, pack_rows([(to_left[i], 7) for i in range(4)] + [(s1[0][0], 6)])),
            (cl_lower, pack_rows([(s1[1][0], 0), (s1[0][0], 0)]))):
        for i, part in enumerate(parts):
            ref[i] = part

    for load in loads[2:]:
        load.wait()
    nz, ny = es_ref.shape[2], es_ref.shape[3]

    def wrapped(field):
        return jnp.concatenate([field, field[:, :16], field[:, ny - 16:]], axis=1)

    es = {(c, p): wrapped(es_ref[c, p]) for c in range(3) for p in range(2)}
    em = {(c, p): wrapped(em_ref[c, p]) for c in range(3) for p in range(2)}
    ns = {p: wrapped(ns_ref[p]) for p in range(2)}
    products = {key: em[key] * es[key] for key in es}
    for i, field in enumerate([products[c, 0] for c in range(3)] + [ns[0]]):
        e_left[i] = field
    e_right[0] = products[0, 1]
    e_next[0] = pack_rows([(field[0:8], 0) for field in [products[key] for key in cells] + [ns[0], ns[1]]])[0]
    e_prev[0] = pack_rows([(products[2, p][nz - 8:], 7) for p in range(2)])[0]
    e_ca[0] = products[2, 0][nz - 8:]
    e_cb[0] = products[0, 1][0:8]

    order = [(c, p) for p in range(2) for c in range(3)]
    sub = sublane((8, 128))
    halos = []
    for t in range(2):
        group = [es[key] for key in order[4 * t:4 * t + 4]]
        group += [group[0]] * (4 - len(group))
        turned = jnp.concatenate(group, axis=0).T
        es_out[:, t] = turned[:ny].reshape(n_gy, 8, 128)
        after = turned[8:ny + 8].reshape(n_gy, 8, 128)
        before = jnp.concatenate([turned[ny - 8:ny], turned[:ny - 8]], axis=0).reshape(n_gy, 8, 128)
        halos.append((after, before))
    column = lax.broadcasted_iota(jnp.int32, (8, 128), 1)
    for k in range(n_gy):
        upper = jnp.where(sub < 4, halos[0][0][k], halos[0][1][k])
        lower = jnp.where(sub < 4, halos[1][0][k], halos[1][1][k])
        spare = jnp.where((sub == 1) | (sub == 2), turn(upper, 2), pltpu.roll(upper, 2 * nz, axis=1))
        spare = jnp.where((sub == 3) | (sub == 4), half_turn(pltpu.roll(lower, 2 * nz, axis=1)), spare)
        es_out[k, 1] = jnp.where(column < 2 * nz, es_out[k, 1], spare)

    pl.semaphore_wait(barrier, len(greeted))

    first = [
        message(cr_upper, in_cl_below, at(1, 1)), message(cr_lower, in_cl_above, at(1, -1)),
        message(cl_upper, in_cr_below, at(-1, 1)), message(cl_lower, in_cr_above, at(-1, -1)),
        message(x_right, in_left, at(1, 0)), message(x_left, in_right, at(-1, 0)),
        message(y_upper, in_below, at(0, 1)), message(y_lower, in_above, at(0, -1)),
    ]
    exchange = []
    for j in [k for k in sorted(range(n_gy), key=lambda j: (abs(j % 4 - 2), -min(j, n_gy - j))) if k]:
        peer = at(0, j)
        exchange.append(message(es_out.at[peer[1]], es_in.at[gy], peer))
    es_in[gy] = es_out[gy]
    edge_halo = [
        message(e_left, in_e_right, at(-1, 0)), message(e_right, in_e_left, at(1, 0)),
        message(e_next, in_e_next, at(0, -1)), message(e_prev, in_e_prev, at(0, 1)),
        message(e_ca, in_e_ca, at(-1, 1)), message(e_cb, in_e_cb, at(1, -1)),
    ]

    for copy in exchange:
        copy.wait_recv()
    lane4 = lax.broadcasted_iota(jnp.int32, (8, 128), 1) // nz
    total = r_ref.shape[3]
    for i, (c, p) in enumerate(order):
        t, q = divmod(i, 4)
        for m in range(total // 128):
            for h in range(2):
                tile = None
                for jj in range(4):
                    piece = es_in[4 * m + jj, 1 if h else t]
                    place = 2 + i % 2 if h else q
                    if jj != place:
                        piece = pltpu.roll(piece, (nz * (jj - place)) % 128, axis=1)
                    tile = piece if tile is None else jnp.where(lane4 == jj, piece, tile)
                faced[p, c, 8 * h:8 * h + 8, 128 * m:128 * m + 128] = turn(tile, -2 * (i // 2)) if h else tile
    for ref, p, comps in ((ef_right, 1, (0, 1, 2)), (ef_left, 0, (1, 2))):
        tile = None
        for i, c in enumerate(comps):
            ref[i] = faced[p, c, 0:8]
            piece = faced[p, c, 8:16]
            piece = pltpu.roll(piece, 2 * i, axis=0) if i else piece
            tile = piece if tile is None else jnp.where((wide == 2 * i) | (wide == 2 * i - 1), piece, tile)
        ref[len(comps)] = tile
    scale_halo = [message(ef_right, in_ef_left, at(1, 0)), message(ef_left, in_ef_right, at(-1, 0))]

    for copy in first:
        copy.wait_recv()

    rr, ff, dd, ss = {}, {}, {}, {}
    for i, (c, p) in enumerate(cells):
        above = c == 1
        rr[c, p] = joined(r_ref[c, p], with_rows(None, (in_below, i, 7), *[(in_above, p, 0)] * above))
        ff[c, p] = joined(fm_ref[c, p], with_rows(None, (in_below, 6 + i, 7), *[(in_above, 2 + p, 0)] * above))
    for c in range(3):
        rr[c, -1] = joined(in_left[c], with_rows(None, (in_cl_above, 0, 0)) if c == 1 else in_left[c])
        ff[c, -1] = joined(in_left[3 + c], with_rows(None, (in_cl_above, 1, 0)) if c == 1 else in_left[3 + c])
    rr[0, 2] = joined(in_right[0], with_rows(None, (in_cr_below, 0, 7)))
    ff[0, 2] = joined(in_right[1], with_rows(None, (in_cr_below, 1, 7)))
    for key in rr:
        dd[key] = ff[key] + 2.0 * grad_div_weight
        ss[key] = damping * rr[key] / dd[key]

    def more_rows(key, *items):
        ss[key] = joined(ss[key][0:8], with_rows(ss[key][8:16], *items))

    for i, (c, p) in enumerate(cells):
        more_rows((c, p), (in_below, 12 + i, 6), (in_above, (4, 8, 6)[c] + p, 1 if c == 1 else 0))
    for c in range(3):
        more_rows((c, -1), (in_cl_below, c, 7), (in_cl_above, (2, 4, 3)[c], 1 if c == 1 else 0))
    more_rows((0, 2), (in_cr_below, 4, 6), (in_cr_above, 1, 0))
    known = joined(in_right[2], with_rows(None, (in_cr_below, 2, 7)))
    second_flux = joined(in_right[3], with_rows(None, (in_cr_below, 3, 7), (in_cr_above, 0, 0)))

    def divergence(u, p):
        return (u[0, p + 1] - u[0, p]) + (up(u[1, p], 0) - u[1, p]) + (up(u[2, p], 1) - u[2, p])

    def apply_faces(u, div, c, p):
        shifted = div[p - 1] if c == 0 else down(div[p], c - 1)
        return ff[c, p] * u[c, p] + grad_div_weight * (shifted - div[p])

    div1 = {p: divergence(ss, p) for p in range(-1, 2)}
    div1[2] = known + (up(second_flux, 0) - second_flux)
    far = in_left[6]
    far = jnp.where(wide == 7, far + turn(in_cl_above[0], 2), far)
    div1[-2] = joined(far, far)
    tt = {key: ss[key] + damping * (rr[key] - apply_faces(ss, div1, *key)) / dd[key] for key in rr}
    div2 = {p: divergence(tt, p) for p in range(-1, 2)}
    res = {(c, p): rr[c, p] - apply_faces(tt, div2, c, p) for c in range(3) for p in range(2)}

    mine = {key: res[key][0:8] for key in res}
    span = nz + 8
    lane = lax.broadcasted_iota(jnp.int32, (8, 128), 1)
    total = r_ref.shape[3]
    for k in range(n_gy):
        for p in range(2):
            tile = None
            for c in range(3):
                shift = (span * c - (nz * k - 4)) % total
                piece = (pltpu.roll(mine[c, p], shift, axis=1) if shift else mine[c, p])[:, :128]
                tile = piece if tile is None else jnp.where(lane >= span * c, piece, tile)
            win[k, p] = tile
    windows = []
    for j in [k for k in sorted(range(n_gy), key=lambda j: (abs(j % 4 - 2), -min(j, n_gy - j))) if k]:
        peer = at(0, j)
        windows.append(message(win.at[peer[1]], in_win.at[gy], peer))
    in_win[gy] = win[gy]

    for ref, parts in (
            (res_right, [mine[1, 0], mine[2, 0], mine[0, 1], mine[1, 1], mine[2, 1]]),
            (res_left, [mine[0, 0], mine[1, 0], mine[2, 0]]),
            (res_upper, pack_rows([(mine[key], 7) for key in cells] + [(mine[c, p], 6) for c in (0, 2) for p in range(2)])),
            (res_lower, pack_rows([(mine[key], 0) for key in cells])),
            (rr_upper, pack_rows([(mine[c, 1], 7) for c in range(3)])),
            (rr_lower, pack_rows([(mine[c, 1], 0) for c in range(3)] + [(mine[1, 0], 0)])),
            (rl_upper, pack_rows([(mine[c, 0], 7) for c in range(3)] + [(mine[0, 0], 6)])),
            (rl_lower, pack_rows([(mine[c, 0], 0) for c in range(2)]))):
        for i, part in enumerate(parts):
            ref[i] = part
    second = [
        message(rr_upper, in_rl_below, at(1, 1)), message(rr_lower, in_rl_above, at(1, -1)),
        message(rl_upper, in_rr_below, at(-1, 1)), message(rl_lower, in_rr_above, at(-1, -1)),
        message(res_right, in_res_left, at(1, 0)), message(res_left, in_res_right, at(-1, 0)),
        message(res_upper, in_res_below, at(0, 1)), message(res_lower, in_res_above, at(0, -1)),
    ]


    for copy in windows:
        copy.wait_recv()
    passed_on = [message(in_win.at[:, 1], in_win_left, at(1, 0)), message(in_win.at[:, 0], in_win_right, at(-1, 0))]
    for copy in edge_halo:
        copy.wait_recv()
    both = {}
    for i, (c, p) in enumerate(cells):
        places = [(in_e_next, i, 0)] + [(in_e_prev, p, 7)] * (c == 2)
        both[c, p] = joined(wrapped(em_ref[c, p]) * wrapped(es_ref[c, p]), with_rows(None, *places))
    node = {p: joined(wrapped(ns_ref[p]), with_rows(None, (in_e_next, 6 + p, 0))) for p in range(2)}
    both[0, -1] = joined(in_e_left[0], in_e_cb[0])
    for c in range(3):
        both[c, 2] = joined(in_e_right[c], in_e_ca[0])
    node[2] = joined(in_e_right[3], in_e_ca[0])
    for copy in second + scale_halo:
        copy.wait_recv()

    def ef_halo(ref, count, i):
        tile = ref[count]
        return joined(ref[i], pltpu.roll(tile, 8 - 2 * i, axis=0) if i else tile)

    for i, (c, p) in enumerate(cells):
        rows = [(in_res_below, i, 7), (in_res_above, i, 0)] + [(in_res_below, 6 + c + p, 6)] * (c != 1)
        res[c, p] = joined(mine[c, p], with_rows(None, *rows))
    res[1, -2] = joined(in_res_left[0], with_rows(None, (in_rl_above, 3, 0)))
    res[2, -2] = joined(in_res_left[1], in_res_left[1])
    for c in range(3):
        res[c, -1] = joined(in_res_left[2 + c], with_rows(None, (in_rl_below, c, 7), (in_rl_above, c, 0)))
        rows = [(in_rr_below, c, 7)] + [(in_rr_below, 3, 6)] * (c == 0) + [(in_rr_above, c, 0)] * (c < 2)
        res[c, 2] = joined(in_res_right[c], with_rows(None, *rows))
    scale = {(c, p): faced[p, c] for c in range(3) for p in range(2)}
    for c in range(3):
        scale[c, -1] = ef_halo(in_ef_left, 3, c)
    for c in range(1, 3):
        scale[c, 2] = ef_halo(in_ef_right, 2, c - 1)
    sm = {key: scale[key] * curl_adjoint(res, *key, FACE) for key in scale}
    new = {key: tt[key] + curl(sm, *key, FACE) for key in tt}
    div3 = {p: divergence(new, p) for p in range(-1, 2)}
    for c in range(3):
        for p in range(2):
            key = (c, p)
            out = new[key] + damping * (rr[key] - apply_faces(new, div3, c, p)) / dd[key]
            vel_ref[c, p] = out[0:8]

    store = [pltpu.make_async_copy(vel_ref, vel_hbm, load_sem.at[5]), pltpu.make_async_copy(ec_ref, ec_hbm, load_sem.at[6])]
    store[0].start()
    for copy in passed_on:
        copy.wait_recv()
    g = {}
    for p, ref in ((-1, in_win_left), (0, None), (1, None), (2, in_win_right)):
        rows = (in_win[:, p] if ref is None else ref[...]).reshape(ny, 128)
        turned = jnp.concatenate([rows, rows[:16], rows[ny - 16:]], axis=0).T
        for c in range(3):
            g[c, p] = pltpu.roll(turned[span * c:span * c + span], span - 4, axis=0)
    edge_residual = {key: curl_adjoint(g, *key, EDGE) for key in both}
    ww = {key: both[key] * edge_residual[key] for key in both}
    pot = {}
    for p in range(3):
        adjoint = ((ww[0, p - 1] - ww[0, p]) + (down(ww[1, p], 1) - ww[1, p])) + (down(ww[2, p], 0) - ww[2, p])
        pot[0, p] = node[p] * -adjoint
    for c in range(3):
        for p in range(2):
            ahead = pot[0, p + 1] if c == 0 else up(pot[0, p], EDGE[c - 1])
            smoothed = wrapped(es_ref[c, p]) * edge_residual[c, p][:nz]
            ec_ref[c, p] = (smoothed + (ahead - pot[0, p])[:nz])[:, :ny]
    store[1].start()
    for copy in sent:
        copy.wait_send()
    for copy in store:
        copy.wait()


def hand_over(a, b, a_out, b_out):
    a_out[...] = a[...]
    b_out[...] = b[...]


def on_device(right_side, face_mass, edge_scale, edge_mass, node_scale):
    n_gx, n_gy = lax.axis_size("gx"), lax.axis_size("gy")
    edge_scale, edge_mass, node_scale = (jnp.swapaxes(a, -1, -2) for a in (edge_scale, edge_mass, node_scale))
    total, nz = right_side.shape[3], edge_scale.shape[2]

    def own(a):
        return pltpu.VMEM(a.shape, jnp.float32)

    def rows(*lead):
        return pltpu.VMEM((*lead, 8, total), jnp.float32)

    def tile(*lead):
        return pltpu.VMEM((*lead, 8, 128), jnp.float32)

    def field(*lead):
        return pltpu.VMEM((*lead, nz, 128), jnp.float32)

    arguments = (right_side, face_mass, edge_scale, edge_mass, node_scale)
    first = [rows(7), rows(4), rows(3), rows(2), rows(1), rows(1), rows(1), rows(1)]
    second = [rows(5), rows(3), rows(2), rows(1), rows(1), rows(1), rows(1), rows(1)]
    halo = [field(4), field(1), tile(1), tile(1), tile(1), tile(1)]
    count = 24 + 5 * n_gy - 2
    velocity, correction = pl.pallas_call(
        functools.partial(kernel, n_gx, n_gy),
        out_shape=(jax.ShapeDtypeStruct(right_side.shape, jnp.float32),
                   jax.ShapeDtypeStruct(edge_scale.shape, jnp.float32)),
        in_specs=[pl.BlockSpec(memory_space=pltpu.HBM)] * 5,
        out_specs=(pl.BlockSpec(memory_space=pl.ANY),) * 2,
        scratch_shapes=[own(a) for a in (*arguments, right_side, edge_scale)] + first + first + [
            tile(n_gy, 2), tile(n_gy, 2), pltpu.VMEM((2, 3, 16, total), jnp.float32),
            rows(4), rows(3), rows(4), rows(3)] + halo + halo + [
            *second, *second, tile(n_gy, 2), tile(n_gy, 2), tile(n_gy), tile(n_gy),
            pltpu.SemaphoreType.DMA((7,)),
            pltpu.SemaphoreType.DMA((count,)), pltpu.SemaphoreType.DMA((count,)),
        ],
        compiler_params=pltpu.CompilerParams(
            collective_id=0, has_side_effects=True, vmem_limit_bytes=60 * 1024 * 1024),
    )(*arguments)
    inside = pl.BlockSpec(memory_space=pltpu.VMEM)
    velocity, correction = pl.pallas_call(
        hand_over,
        out_shape=(jax.ShapeDtypeStruct(velocity.shape, jnp.float32),
                   jax.ShapeDtypeStruct(correction.shape, jnp.float32)),
        in_specs=[inside, inside],
        out_specs=(inside, inside),
        compiler_params=pltpu.CompilerParams(vmem_limit_bytes=60 * 1024 * 1024),
    )(velocity, correction)
    return velocity, jnp.swapaxes(correction, 2, 3)


def solution(mesh):
    placed = (
        P(None, "gx", "gy", None),
        P(None, "gx", "gy", None),
        P(None, "gx", None, "gy"),
        P(None, "gx", None, "gy"),
        P("gx", None, "gy"),
    )
    return jax.shard_map(
        on_device,
        mesh=mesh,
        in_specs=placed,
        out_specs=(P(None, "gx", "gy", None), P(None, "gx", None, "gy")),
        check_vma=False,
    )
```
